128 devices in a mesh: section: 16 (over x_lo, y, core), island: 8 (over x_hi, z).
Axes of the slice: x: 4 (x_hi: 2, x_lo: 2; x = x_hi * 2 + x_lo), y: 4, z: 4, core: 2. Of those that a mesh axis runs over, the one named last changes fastest.
Arguments:
- inputs: bfloat16 [8, 512, 16384], P('island', None, 'section'), may hold values from -6 to 6
- gate_pre: bfloat16 [8, 512, 3328], P('island', 'section'), may hold values from -6 to 6
- up_cot: bfloat16 [8, 512, 3328], P('island', 'section'), may hold values from -6 to 6
- weights: bfloat16 [8, 16384, 3328], P('island', 'section'), may hold values from -0.0625 to 0.0625
- outer: float32 [16384, 3328], P(('section', 'island')), may hold values from -0.6 to 0.6
- momentum: float32 [16384, 3328], P(('section', 'island')), may hold values from -0.6 to 0.6
Outputs:
- input_grad: bfloat16 [8, 512, 16384], P('island', None, 'section')
- gate_grad: bfloat16 [8, 512, 3328], P('island', 'section')
- new_weights: bfloat16 [16384, 3328], P('section')
- new_outer: float32 [16384, 3328], P(('section', 'island'))
- new_momentum: float32 [16384, 3328], P(('section', 'island'))
The draws below stay inside these ranges and needn't reach their ends.
All inputs are finite; a program needn't handle non-finite values.
Results may differ from the reference program's by a relative error of at most 0.01.
Values may be sent and summed in bfloat16 or wider, within the bound.
A program may use at most 128 MiB of HBM per device.

```python
import jax
import jax.numpy as jnp
from jax import lax

D = 16384
FS = 3328
TOK = 512
N_ISLAND = 8


def with_spikes(entries, rng, source, target, parts, factor):
    def block_of(axis_at):
        return (jnp.arange(entries.shape[axis_at]) // (entries.shape[axis_at] // parts)).reshape((-1,) + (1,) * (entries.ndim - 1 - axis_at))

    near = jax.random.permutation(rng, parts)[block_of(target)]
    other_side = (block_of(target) + parts // 2) % parts
    return jnp.where((block_of(source) == near) | (block_of(source) == other_side), factor * entries, entries)


def block_scale(stream_key, shape, cuts, smallest, largest):
    level = 1.0
    for dim, blocks in cuts:
        draws = jax.random.uniform(jax.random.fold_in(jax.random.fold_in(stream_key, 6), dim), (blocks,), jnp.float32, smallest / len(cuts), largest / len(cuts))
        level = level * jnp.repeat(jnp.exp(draws), shape[dim] // blocks).reshape((-1,) + (1,) * (len(shape) - 1 - dim))
    return level


def gaussian(own_key, shape, spread, bound, pieces=(), dtype=jnp.bfloat16):
    drawn = spread * jax.random.normal(own_key, shape, jnp.float32)
    if pieces:
        drawn = drawn * block_scale(own_key, shape, pieces, -0.22, 0.18)
    return jnp.clip(drawn, -bound, bound).astype(dtype)


def bell_draw_with(rng, shape, deviation, most, cuts, heavy, held_as=jnp.bfloat16):
    drawn = deviation * jax.random.normal(rng, shape, jnp.float32)
    if cuts:
        drawn = drawn * block_scale(rng, shape, cuts, -0.22, 0.18)
    return jnp.clip(with_spikes(drawn, jax.random.fold_in(rng, 3), *heavy), -most, most).astype(held_as)


def setup_inputs(seed: int = 0) -> dict:
    key_list = jax.random.split(jax.random.key(seed), 7)
    inputs = gaussian(key_list[0], (N_ISLAND, TOK, D), 1.0, 6.0, ((0, 8), (2, 16)))
    gate_pre = gaussian(key_list[1], (N_ISLAND, TOK, FS), 1.0, 6.0, ((0, 8), (1, 16)))
    up_cot = gaussian(key_list[2], (N_ISLAND, TOK, FS), 1.0, 6.0, ((0, 8), (1, 16)))
    weights = bell_draw_with(key_list[3], (N_ISLAND, D, FS), D ** -0.5, 0.0625, ((0, 8), (1, 16)), (0, 1, 8, 2.0))
    outer = gaussian(key_list[4], (D, FS), 0.1, 0.6, ((0, 128),), jnp.float32)
    momentum = gaussian(key_list[5], (D, FS), 0.1, 0.6, ((0, 128),), jnp.float32)
    return {"inputs": inputs, "gate_pre": gate_pre, "up_cot": up_cot, "weights": weights, "outer": outer, "momentum": momentum}


inner_rate = 0.0005
outer_rate = 0.7
nesterov_mu = 0.9


def contract_rows(left_rows, right_rows):
    return lax.dot_general(left_rows, right_rows, (((0,), (0,)), ((), ())), preferred_element_type=jnp.float32)


def reference(inputs, gate_pre, up_cot, weights, outer, momentum):
    island_total = jnp.zeros((D, FS), jnp.float32)
    input_list = []
    gate_list = []
    for island in range(N_ISLAND):
        features = inputs[island]
        weight = weights[island]
        gate_full = gate_pre[island].astype(jnp.float32)
        cot_full = up_cot[island].astype(jnp.float32)
        up_full = jnp.dot(features, weight, preferred_element_type=jnp.float32)
        gate_sigma = jax.nn.sigmoid(gate_full)
        gate_list.append((cot_full * up_full * gate_sigma * (1.0 + gate_full * (1.0 - gate_sigma))).astype(jnp.bfloat16))
        d_up = (cot_full * gate_full * gate_sigma).astype(jnp.bfloat16)
        pulled_back = lax.dot_general(d_up, weight, (((1,), (1,)), ((), ())), preferred_element_type=jnp.float32)
        input_list.append(pulled_back.astype(jnp.bfloat16))
        weight_grad = contract_rows(features, d_up)
        inner_block = (weight.astype(jnp.float32) - inner_rate * weight_grad).astype(jnp.bfloat16)
        island_total = island_total + lax.optimization_barrier(inner_block).astype(jnp.float32)
    mean_inner = island_total / N_ISLAND
    delta_rows = outer - mean_inner
    new_momentum = nesterov_mu * momentum + delta_rows
    new_outer = outer - outer_rate * (delta_rows + nesterov_mu * new_momentum)
    return (jnp.stack(input_list), jnp.stack(gate_list), new_outer.astype(jnp.bfloat16), new_outer, new_momentum)
```

```python
import jax
import jax.numpy as jnp
from jax import lax
from jax.sharding import PartitionSpec as P

inner_rate = 0.0005
outer_rate = 0.7
nesterov_mu = 0.9


def contract_rows(left_rows, right_rows):
    return lax.dot_general(
        left_rows, right_rows, (((0,), (0,)), ((), ())), preferred_element_type=jnp.float32
    )


def gated_grad(shard_piece):
    gate_piece = shard_piece[0].astype(jnp.float32)
    return (shard_piece[1].astype(jnp.float32) * gate_piece * jax.nn.sigmoid(gate_piece)).astype(
        jnp.bfloat16
    )


def local(inputs, gate_pre, up_cot, weights, outer, momentum):
    features = inputs[0]
    gate_mine = gate_pre[0]
    cot_mine = up_cot[0]
    weight = weights[0]
    row_block = features
    up_mine = lax.psum_scatter(
        jnp.dot(row_block, weight, preferred_element_type=jnp.float32).astype(jnp.bfloat16),
        "section",
        scatter_dimension=0,
        tiled=True,
    ).astype(jnp.float32)
    gate_full = gate_mine.astype(jnp.float32)
    gate_sigma = jax.nn.sigmoid(gate_full)
    gate_grad = (
        cot_mine.astype(jnp.float32) * up_mine * gate_sigma * (1.0 + gate_full * (1.0 - gate_sigma))
    ).astype(jnp.bfloat16)
    d_up = lax.all_gather(gated_grad((gate_mine, cot_mine)), "section", axis=0, tiled=True)
    row_block = features
    weight_grad = contract_rows(row_block, d_up)
    pulled_back = lax.dot_general(
        d_up, weight, (((1,), (1,)), ((), ())), preferred_element_type=jnp.float32
    )
    input_grad = pulled_back.astype(jnp.bfloat16)
    inner_block = weight.astype(jnp.float32) - inner_rate * weight_grad
    summed = lax.psum_scatter(
        inner_block.astype(jnp.bfloat16), "island", scatter_dimension=0, tiled=True
    ).astype(jnp.float32)
    mean_inner = summed / lax.axis_size("island")
    delta_rows = outer - mean_inner
    moment = nesterov_mu * momentum + delta_rows
    updated = outer - outer_rate * (delta_rows + nesterov_mu * moment)
    gathered = lax.all_gather(updated.astype(jnp.bfloat16), "island", axis=0, tiled=True)
    return (input_grad[None], gate_grad[None], gathered, updated, moment)


def solution(mesh):
    placed = (
        P("island", None, "section"),
        P("island", "section", None),
        P("island", "section", None),
        P("island", "section", None),
        P(("section", "island"), None),
        P(("section", "island"), None),
    )
    return jax.shard_map(
        local,
        mesh=mesh,
        in_specs=placed,
        out_specs=(
            P("island", None, "section"),
            P("island", "section", None),
            P("section", None),
            P(("section", "island"), None),
            P(("section", "island"), None),
        ),
        check_vma=False,
    )
```

```python
import functools

import jax
import jax.numpy as jnp
from jax import lax
from jax.experimental import pallas as pl
from jax.experimental.pallas import tpu as pltpu
from jax.sharding import PartitionSpec as P

inner_rate = 0.0005
outer_rate = 0.7
nesterov_mu = 0.9

MESH = pl.DeviceIdType.MESH
F32 = jnp.float32
BF16 = jnp.bfloat16

W = 256
N_Z = 4
N_ISL = 8
PLANE = 8
TB = 32
RB = 128
LAG = 6


def kernel(
    n_chunk,
    x_hbm, gate_hbm, cot_hbm, w_hbm, outer_hbm, mom_hbm,
    ig_out, gg_out, nw_out, no_out, nm_out,
    x_v, xt_v, gate_v, cot_v, outer_v, mom_v, w_v, dup_v,
    inner_v, r1_v, r2_v, xs_v, rx_v,
    ups_v, upr_v, upo_v, upt_v, upp_v, acc_v,
    in_sem, w_sem, snd, r_dup, r_sib, r_s1, r_raw, r_acc, r_x,
    r_gx, r_go, r_gp, r_gf, r_ups, r_upp,
):
    sec = lax.axis_index("section")
    isl = lax.axis_index("island")
    core = lax.rem(sec, 2)
    place = sec // 2
    z = lax.rem(isl, N_Z)
    xh = isl // N_Z
    up_z = lax.rem(z + 1, N_Z)
    dn_z = lax.rem(z + N_Z - 1, N_Z)
    op_z = lax.rem(z + 2, N_Z)
    to_up = (sec, xh * N_Z + up_z)
    to_dn = (sec, xh * N_Z + dn_z)
    to_x = (sec, (1 - xh) * N_Z + z)
    to_sib = (place * 2 + 1 - core, isl)

    def peer(k):
        return (lax.rem(place + k, PLANE) * 2 + core, isl)

    def remote(src, dst, c, recv, device):
        return pltpu.make_async_remote_copy(
            src_ref=src, dst_ref=dst, send_sem=snd.at[c], recv_sem=recv,
            device_id=device, device_id_type=MESH,
        )

    def arrived(dst, recv):
        pltpu.make_async_copy(dst, dst, recv).wait()

    def cols(c):
        return pl.ds(pl.multiple_of(c * W, W), W)

    barrier = pltpu.get_barrier_semaphore()
    for device in (to_up, to_dn, to_x, to_sib):
        pl.semaphore_signal(barrier, inc=1, device_id=device, device_id_type=MESH)
    for k in range(1, PLANE):
        pl.semaphore_signal(barrier, inc=1, device_id=peer(k), device_id_type=MESH)

    def w_copy(c):
        return pltpu.make_async_copy(w_hbm.at[:, :, cols(c)], w_v.at[c], w_sem.at[c])

    in_copies = [
        pltpu.make_async_copy(gate_hbm, gate_v, in_sem.at[0]),
        pltpu.make_async_copy(cot_hbm, cot_v, in_sem.at[1]),
        pltpu.make_async_copy(x_hbm.at[:, 0], x_v.at[0], in_sem.at[2]),
        pltpu.make_async_copy(x_hbm.at[:, 1], x_v.at[1], in_sem.at[3]),
        pltpu.make_async_copy(outer_hbm, outer_v, in_sem.at[4]),
        pltpu.make_async_copy(mom_hbm, mom_v, in_sem.at[5]),
    ]
    for copy in in_copies[:4]:
        copy.start()

    def dup_form(c):
        g = gate_v[:, cols(c)].astype(F32)
        s = jax.nn.sigmoid(g)
        d = cot_v[:, cols(c)].astype(F32) * g * s
        dup_v[c * 16 + core * PLANE + place] = d.astype(BF16)

    def dup_send(c):
        mine = dup_v.at[c * 16 + core * PLANE + place]
        for k in range(1, PLANE):
            remote(mine, mine, c, r_dup.at[c], peer(k)).start()

    def dup_share(c):
        arrived(dup_v.at[pl.ds(c * 16 + core * PLANE, PLANE - 1)], r_dup.at[c])
        half = dup_v.at[pl.ds(c * 16 + core * PLANE, PLANE)]
        remote(half, half, c, r_sib.at[c], to_sib).start()

    def inner_form(c):
        arrived(dup_v.at[pl.ds(c * 16 + (1 - core) * PLANE, PLANE)], r_sib.at[c])
        d_up = dup_v[pl.ds(c * 16, 16)].reshape(16 * TB, W)
        for half in range(2):
            lhs = xt_v[half].reshape(N_Z * RB, 16 * TB)
            grad = jnp.dot(lhs, d_up, preferred_element_type=F32)
            for rel in range(N_Z):
                block = half * N_Z + lax.rem(z + rel, N_Z)
                w_part = w_v[c, block].astype(F32)
                inner_v[c, half, rel] = (
                    w_part - inner_rate * grad[rel * RB : (rel + 1) * RB]
                ).astype(BF16)
        remote(inner_v.at[c, 0, 2], r1_v.at[c, 0], c, r_s1.at[c, 0], to_up).start()
        remote(inner_v.at[c, 1, 2], r1_v.at[c, 1], c, r_s1.at[c, 1], to_dn).start()
        remote(inner_v.at[c, 1, 1], r2_v.at[c, 0, 1], c, r_raw.at[c, 0], to_up).start()
        remote(inner_v.at[c, 0, 3], r2_v.at[c, 1, 0], c, r_raw.at[c, 1], to_dn).start()

    def rs_second(c):
        arrived(r1_v.at[c, 0], r_s1.at[c, 0])
        inner_v[c, 0, 1] = (inner_v[c, 0, 1].astype(F32) + r1_v[c, 0].astype(F32)).astype(BF16)
        remote(inner_v.at[c, 0, 1], r2_v.at[c, 0, 0], c, r_acc.at[c, 0], to_up).start()
        arrived(r1_v.at[c, 1], r_s1.at[c, 1])
        inner_v[c, 1, 3] = (inner_v[c, 1, 3].astype(F32) + r1_v[c, 1].astype(F32)).astype(BF16)
        remote(inner_v.at[c, 1, 3], r2_v.at[c, 1, 1], c, r_acc.at[c, 1], to_dn).start()

    def rs_x(c):
        arrived(r2_v.at[c, 0, 1], r_raw.at[c, 0])
        arrived(r2_v.at[c, 1, 0], r_raw.at[c, 1])
        arrived(r2_v.at[c, 0, 0], r_acc.at[c, 0])
        arrived(r2_v.at[c, 1, 1], r_acc.at[c, 1])
        xs_v[c] = (
            inner_v[c, 1 - xh, 0].astype(F32)
            + r2_v[c, 0, 1 - xh].astype(F32)
            + r2_v[c, 1, 1 - xh].astype(F32)
        ).astype(BF16)
        remote(xs_v.at[c], rx_v.at[c], c, r_x.at[c], to_x).start()

    def block_of(c, half, zz):
        return nw_out.at[half * N_Z + zz, :, cols(c)]

    def update(c):
        arrived(rx_v.at[c], r_x.at[c])
        total = (
            inner_v[c, xh, 0].astype(F32)
            + r2_v[c, 0, xh].astype(F32)
            + r2_v[c, 1, xh].astype(F32)
            + rx_v[c].astype(F32)
        )
        own = outer_v[:, cols(c)]
        delta = own - total * (1.0 / N_ISL)
        moment = nesterov_mu * mom_v[:, cols(c)] + delta
        new = own - outer_rate * (delta + nesterov_mu * moment)
        nm_out[:, cols(c)] = moment
        no_out[:, cols(c)] = new
        nw_out[isl, :, cols(c)] = new.astype(BF16)
        mine = block_of(c, xh, z)
        remote(mine, mine, c, r_gx.at[c], to_x).start()
        remote(mine, mine, c, r_go.at[c, 0], to_up).start()
        remote(mine, mine, c, r_go.at[c, 1], to_dn).start()

    def ag_partner(c):
        theirs = block_of(c, 1 - xh, z)
        arrived(theirs, r_gx.at[c])
        remote(theirs, theirs, c, r_gp.at[c, 0], to_up).start()
        remote(theirs, theirs, c, r_gp.at[c, 1], to_dn).start()

    def ag_forward(c):
        arrived(block_of(c, xh, dn_z), r_go.at[c, 0])
        arrived(block_of(c, 1 - xh, dn_z), r_gp.at[c, 0])
        low = block_of(c, 0, dn_z)
        remote(low, low, c, r_gf.at[c, 0], to_up).start()
        arrived(block_of(c, xh, up_z), r_go.at[c, 1])
        arrived(block_of(c, 1 - xh, up_z), r_gp.at[c, 1])
        high = block_of(c, 1, up_z)
        remote(high, high, c, r_gf.at[c, 1], to_dn).start()

    def ag_last(c):
        arrived(block_of(c, 0, op_z), r_gf.at[c, 0])
        arrived(block_of(c, 1, op_z), r_gf.at[c, 1])

    def up_form(c):
        w_all = w_v[c].reshape(N_ISL * RB, W)
        lhs = x_v[1 - core].reshape(PLANE * TB, N_ISL * RB)
        ups_v[c] = jnp.dot(lhs, w_all, preferred_element_type=F32).astype(BF16)
        remote(ups_v.at[c], upr_v.at[c], c, r_ups.at[c], to_sib).start()
        lhs = x_v[core].reshape(PLANE * TB, N_ISL * RB)
        upo_v[c] = jnp.dot(lhs, w_all, preferred_element_type=F32).astype(BF16)

    def up_add(c):
        arrived(upr_v.at[c], r_ups.at[c])
        both = upo_v[c].astype(F32) + upr_v[c].astype(F32)
        upt_v[pl.ds(c * PLANE, PLANE)] = both.astype(BF16).reshape(PLANE, TB, W)
        for k in range(1, PLANE):
            to = lax.rem(place + k, PLANE)
            remote(
                upt_v.at[c * PLANE + to], upp_v.at[c * PLANE + place], c, r_upp.at[c], peer(k)
            ).start()

    def up_last(c):
        arrived(upp_v.at[pl.ds(c * PLANE, PLANE - 1)], r_upp.at[c])
        up = upt_v[c * PLANE + place].astype(F32)
        for k in range(1, PLANE):
            up = up + upp_v[c * PLANE + lax.rem(place + k, PLANE)].astype(F32)
        g = gate_v[:, cols(c)].astype(F32)
        s = jax.nn.sigmoid(g)
        out = cot_v[:, cols(c)].astype(F32) * up * s * (1.0 + g * (1.0 - s))
        gg_out[:, cols(c)] = out.astype(BF16)

    def ig_form(c):
        d_up = dup_v[pl.ds(c * 16, 16)].reshape(16 * TB, W)
        w_all = w_v[c].reshape(N_ISL * RB, W)
        part = lax.dot_general(
            d_up, w_all, (((1,), (1,)), ((), ())), preferred_element_type=F32
        )
        acc_v[...] += part

    in_copies[0].wait()
    in_copies[1].wait()
    w_copy(0).start()
    dup_form(0)
    pl.semaphore_wait(barrier, 3 + PLANE)
    dup_send(0)

    @pl.loop(1, 3)
    def _(c):
        dup_form(c)
        dup_send(c)

    @pl.loop(1, n_chunk)
    def _(c):
        w_copy(c).start()

    in_copies[4].start()
    in_copies[5].start()
    in_copies[2].wait()
    in_copies[3].wait()
    for block in range(N_ISL):
        piece = x_v[:, :, :, block * RB : (block + 1) * RB].reshape(16 * TB, RB)
        rel = lax.rem(block % N_Z + N_Z - z, N_Z)
        xt_v[block // N_Z, rel] = piece.T
    acc_v[...] = jnp.zeros_like(acc_v)
    dup_share(0)

    def at(c, lo, hi, *steps):
        @pl.when((c >= lo) & (c < hi))
        def _():
            for step in steps:
                step(c)

    @pl.loop(0, n_chunk + LAG)
    def _(t):
        def first(c):
            dup_form(c)
            dup_send(c)

        at(t + 3, 0, n_chunk, first)
        at(t + 1, 0, n_chunk, dup_share)

        def second(c):
            w_copy(c).wait()
            inner_form(c)
            up_form(c)

        at(t, 0, n_chunk, second)
        at(t - 1, 0, n_chunk, rs_second)
        at(t - 2, 0, n_chunk, rs_x)

        @pl.when(t == 3)
        def _():
            in_copies[4].wait()
            in_copies[5].wait()

        at(t - 3, 0, n_chunk, update)
        at(t - 4, 0, n_chunk, ag_partner)
        at(t - 5, 0, n_chunk, ag_forward)
        at(t, 0, n_chunk, ig_form)
        at(t - 2, 0, n_chunk, up_add)
        at(t - 5, 0, n_chunk, up_last)
        at(t - 6, 0, n_chunk, ag_last)

    for half in range(2):
        ig_out[:, half] = acc_v[half * PLANE * TB : (half + 1) * PLANE * TB].astype(BF16).reshape(
            PLANE, TB, N_ISL * RB
        )

    sent = (2 * 7 * TB + 2 * PLANE * TB + 6 * RB + RB + 3 * RB + 2 * RB + 2 * RB) // TB

    @pl.loop(0, n_chunk)
    def _(c):
        arrived(dup_v.at[pl.ds(0, sent)], snd.at[c])


def local(inputs, gate_pre, up_cot, weights, outer, momentum):
    d_loc, fs = weights.shape[1], weights.shape[2]
    tok = inputs.shape[1]
    c = fs // W
    dma = pltpu.SemaphoreType.DMA
    vmem = pl.BlockSpec(memory_space=pltpu.VMEM)
    hbm = pl.BlockSpec(memory_space=pltpu.HBM)
    ig, gg, nw, no, nm = pl.pallas_call(
        functools.partial(kernel, c),
        out_shape=(
            jax.ShapeDtypeStruct((PLANE, 2, TB, d_loc), BF16),
            jax.ShapeDtypeStruct((TB, fs), BF16),
            jax.ShapeDtypeStruct((N_ISL, RB, fs), BF16),
            jax.ShapeDtypeStruct((RB, fs), F32),
            jax.ShapeDtypeStruct((RB, fs), F32),
        ),
        in_specs=[hbm] * 6,
        out_specs=(vmem,) * 5,
        scratch_shapes=[
            pltpu.VMEM((2, PLANE, TB, d_loc), BF16),
            pltpu.VMEM((2, N_Z, RB, tok), BF16),
            pltpu.VMEM((TB, fs), BF16),
            pltpu.VMEM((TB, fs), BF16),
            pltpu.VMEM((RB, fs), F32),
            pltpu.VMEM((RB, fs), F32),
            pltpu.VMEM((c, N_ISL, RB, W), BF16),
            pltpu.VMEM((c * 16, TB, W), BF16),
            pltpu.VMEM((c, 2, N_Z, RB, W), BF16),
            pltpu.VMEM((c, 2, RB, W), BF16),
            pltpu.VMEM((c, 2, 2, RB, W), BF16),
            pltpu.VMEM((c, RB, W), BF16),
            pltpu.VMEM((c, RB, W), BF16),
            pltpu.VMEM((c, PLANE * TB, W), BF16),
            pltpu.VMEM((c, PLANE * TB, W), BF16),
            pltpu.VMEM((c, PLANE * TB, W), BF16),
            pltpu.VMEM((c * PLANE, TB, W), BF16),
            pltpu.VMEM((c * PLANE, TB, W), BF16),
            pltpu.VMEM((tok, d_loc), F32),
            dma((6,)),
            dma((c,)),
            dma((c,)),
            dma((c,)),
            dma((c,)),
            dma((c, 2)),
            dma((c, 2)),
            dma((c, 2)),
            dma((c,)),
            dma((c,)),
            dma((c, 2)),
            dma((c, 2)),
            dma((c, 2)),
            dma((c,)),
            dma((c,)),
        ],
        compiler_params=pltpu.CompilerParams(
            collective_id=0, has_side_effects=True, vmem_limit_bytes=48 * 2**20
        ),
        cost_estimate=pl.CostEstimate(
            flops=6 * tok * d_loc * fs, bytes_accessed=8 * d_loc * fs, transcendentals=0
        ),
    )(
        inputs.reshape(PLANE, 2, TB, d_loc),
        gate_pre[0],
        up_cot[0],
        weights.reshape(N_ISL, RB, fs),
        outer,
        momentum,
    )
    return (
        ig.reshape(1, tok, d_loc),
        gg[None],
        nw.reshape(d_loc, fs),
        no,
        nm,
    )


def solution(mesh):
    placed = (
        P("island", None, "section"),
        P("island", "section", None),
        P("island", "section", None),
        P("island", "section", None),
        P(("section", "island"), None),
        P(("section", "island"), None),
    )
    return jax.shard_map(
        local,
        mesh=mesh,
        in_specs=placed,
        out_specs=(
            P("island", None, "section"),
            P("island", "section", None),
            P("section", None),
            P(("section", "island"), None),
            P(("section", "island"), None),
        ),
        check_vma=False,
    )
```

```python
import functools

import jax
import jax.numpy as jnp
from jax import lax
from jax.experimental import pallas as pl
from jax.experimental.pallas import tpu as pltpu
from jax.sharding import PartitionSpec as P

inner_rate = 0.0005
outer_rate = 0.7
nesterov_mu = 0.9

MESH = pl.DeviceIdType.MESH
F32 = jnp.float32
BF16 = jnp.bfloat16

W = 256
N_Z = 4
N_ISL = 8
PLANE = 8
TB = 32
RB = 128
HB = RB // 2
X_EVERY, X_AT = 4, 1
LAG_A, LAG_B, LAG_C, LAG_D, LAG_E, LAG_F = 1, 2, 3, 4, 5, 6
LAG_UA, LAG_UB = 2, 5


def kernel(
    n_chunk,
    x_hbm, gate_hbm, cot_hbm, w_hbm, outer_hbm, mom_hbm,
    ig_out, gg_out, nw_out, no_out, nm_out,
    x_v, xt_v, gate_v, cot_v, outer_v, mom_v, w_v, dup_v,
    inner_v, r1_v, r2_v, xs_v, rx_v, rxx_v,
    ups_v, upr_v, upo_v, upt_v, upp_v, acc_v,
    in_sem, w_sem, snd, r_dup, r_sib, r_s1, r_raw, r_acc, r_x,
    r_gx, r_go, r_gp, r_gf, r_gz, r_ups, r_upp,
):
    sec = lax.axis_index("section")
    isl = lax.axis_index("island")
    core = lax.rem(sec, 2)
    place = sec // 2
    z = lax.rem(isl, N_Z)
    xh = isl // N_Z
    up_z = lax.rem(z + 1, N_Z)
    dn_z = lax.rem(z + N_Z - 1, N_Z)
    op_z = lax.rem(z + 2, N_Z)
    to_up = (sec, xh * N_Z + up_z)
    to_dn = (sec, xh * N_Z + dn_z)
    to_x = (sec, (1 - xh) * N_Z + z)
    to_sib = (place * 2 + 1 - core, isl)

    def peer(k):
        return (lax.rem(place + k, PLANE) * 2 + core, isl)

    def remote(src, dst, c, recv, device):
        return pltpu.make_async_remote_copy(
            src_ref=src, dst_ref=dst, send_sem=snd.at[c], recv_sem=recv,
            device_id=device, device_id_type=MESH,
        )

    def arrived(dst, recv):
        pltpu.make_async_copy(dst, dst, recv).wait()

    def cols(c):
        return pl.ds(pl.multiple_of(c * W, W), W)

    barrier = pltpu.get_barrier_semaphore()
    for device in (to_up, to_dn, to_x, to_sib):
        pl.semaphore_signal(barrier, inc=1, device_id=device, device_id_type=MESH)
    for k in range(1, PLANE):
        pl.semaphore_signal(barrier, inc=1, device_id=peer(k), device_id_type=MESH)

    def w_copy(c):
        return pltpu.make_async_copy(w_hbm.at[:, :, cols(c)], w_v.at[c], w_sem.at[c])

    in_copies = [
        pltpu.make_async_copy(gate_hbm, gate_v, in_sem.at[0]),
        pltpu.make_async_copy(cot_hbm, cot_v, in_sem.at[1]),
        pltpu.make_async_copy(x_hbm.at[:, 0], x_v.at[0], in_sem.at[2]),
        pltpu.make_async_copy(x_hbm.at[:, 1], x_v.at[1], in_sem.at[3]),
        pltpu.make_async_copy(outer_hbm, outer_v, in_sem.at[4]),
        pltpu.make_async_copy(mom_hbm, mom_v, in_sem.at[5]),
    ]
    for copy in in_copies[:4]:
        copy.start()

    def dup_form(c):
        g = gate_v[:, cols(c)].astype(F32)
        s = jax.nn.sigmoid(g)
        d = cot_v[:, cols(c)].astype(F32) * g * s
        dup_v[c * 16 + core * PLANE + place] = d.astype(BF16)

    def dup_send(c):
        mine = dup_v.at[c * 16 + core * PLANE + place]
        for k in range(1, PLANE):
            remote(mine, mine, c, r_dup.at[c], peer(k)).start()

    def dup_share(c):
        arrived(dup_v.at[pl.ds(c * 16 + core * PLANE, PLANE - 1)], r_dup.at[c])
        half = dup_v.at[pl.ds(c * 16 + core * PLANE, PLANE)]
        remote(half, half, c, r_sib.at[c], to_sib).start()

    def inner_form(c):
        arrived(dup_v.at[pl.ds(c * 16 + (1 - core) * PLANE, PLANE)], r_sib.at[c])
        d_up = dup_v[pl.ds(c * 16, 16)].reshape(16 * TB, W)
        for half in (1 - xh, xh):
            lhs = xt_v[half].reshape(N_Z * RB, 16 * TB)
            grad = jnp.dot(lhs, d_up, preferred_element_type=F32)
            for rel in range(N_Z):
                block = half * N_Z + lax.rem(z + rel, N_Z)
                w_part = w_v[c, block].astype(F32)
                inner_v[c, half, rel] = (
                    w_part - inner_rate * grad[rel * RB : (rel + 1) * RB]
                ).astype(BF16)

    def add_into(dst, other):
        dst[...] = (dst[...].astype(F32) + other[...].astype(F32)).astype(BF16)

    def z_first(c):
        remote(inner_v.at[c, 0, 2], r1_v.at[c, 0], c, r_s1.at[c, 0], to_up).start()
        remote(inner_v.at[c, 1, 2], r1_v.at[c, 1], c, r_s1.at[c, 1], to_dn).start()
        remote(inner_v.at[c, 1, 1], r2_v.at[c, 0, 1], c, r_raw.at[c, 0], to_up).start()
        remote(inner_v.at[c, 0, 3], r2_v.at[c, 1, 0], c, r_raw.at[c, 1], to_dn).start()

    def z_second(c):
        arrived(r1_v.at[c, 0], r_s1.at[c, 0])
        add_into(inner_v.at[c, 0, 1], r1_v.at[c, 0])
        remote(inner_v.at[c, 0, 1], r2_v.at[c, 0, 0], c, r_acc.at[c, 0], to_up).start()
        arrived(r1_v.at[c, 1], r_s1.at[c, 1])
        add_into(inner_v.at[c, 1, 3], r1_v.at[c, 1])
        remote(inner_v.at[c, 1, 3], r2_v.at[c, 1, 1], c, r_acc.at[c, 1], to_dn).start()

    def z_third(c):
        arrived(r2_v.at[c, 0, 1], r_raw.at[c, 0])
        arrived(r2_v.at[c, 1, 0], r_raw.at[c, 1])
        arrived(r2_v.at[c, 0, 0], r_acc.at[c, 0])
        arrived(r2_v.at[c, 1, 1], r_acc.at[c, 1])
        xs_v[c] = (
            inner_v[c, 1 - xh, 0].astype(F32)
            + r2_v[c, 0, 1 - xh].astype(F32)
            + r2_v[c, 1, 1 - xh].astype(F32)
        ).astype(BF16)
        remote(xs_v.at[c], rx_v.at[c], c, r_x.at[c], to_x).start()

    def x_first(c):
        remote(inner_v.at[c, 1 - xh], rxx_v.at[c // X_EVERY], c, r_x.at[c], to_x).start()

    def x_second(c):
        got = rxx_v.at[c // X_EVERY]
        arrived(got, r_x.at[c])
        low, high = pl.ds(0, HB), pl.ds(HB, HB)
        far, above, below = (inner_v.at[c, xh, rel] for rel in (2, 1, 3))
        add_into(far, got.at[2])
        remote(far.at[low], r1_v.at[c, 0, low], c, r_s1.at[c, 0], to_up).start()
        remote(far.at[high], r1_v.at[c, 1, low], c, r_s1.at[c, 1], to_dn).start()
        add_into(above, got.at[1])
        remote(above.at[high], r2_v.at[c, 0, 0, high], c, r_raw.at[c, 0], to_up).start()
        add_into(below, got.at[3])
        remote(below.at[low], r2_v.at[c, 1, 0, low], c, r_raw.at[c, 1], to_dn).start()

    def x_third(c):
        low, high = pl.ds(0, HB), pl.ds(HB, HB)
        arrived(r1_v.at[c, 0, low], r_s1.at[c, 0])
        above = inner_v.at[c, xh, 1, low]
        add_into(above, r1_v.at[c, 0, low])
        remote(above, r2_v.at[c, 0, 0, low], c, r_acc.at[c, 0], to_up).start()
        arrived(r1_v.at[c, 1, low], r_s1.at[c, 1])
        below = inner_v.at[c, xh, 3, high]
        add_into(below, r1_v.at[c, 1, low])
        remote(below, r2_v.at[c, 1, 0, high], c, r_acc.at[c, 1], to_dn).start()

    def block_of(c, half, zz):
        return nw_out.at[half * N_Z + zz, :, cols(c)]

    def update(c, total):
        own = outer_v[:, cols(c)]
        delta = own - total * (1.0 / N_ISL)
        moment = nesterov_mu * mom_v[:, cols(c)] + delta
        new = own - outer_rate * (delta + nesterov_mu * moment)
        nm_out[:, cols(c)] = moment
        no_out[:, cols(c)] = new
        nw_out[isl, :, cols(c)] = new.astype(BF16)
        mine = block_of(c, xh, z)
        remote(mine, mine, c, r_gx.at[c], to_x).start()
        remote(mine, mine, c, r_go.at[c, 0], to_up).start()
        remote(mine, mine, c, r_go.at[c, 1], to_dn).start()

    def z_update(c):
        arrived(rx_v.at[c], r_x.at[c])
        update(
            c,
            inner_v[c, xh, 0].astype(F32)
            + r2_v[c, 0, xh].astype(F32)
            + r2_v[c, 1, xh].astype(F32)
            + rx_v[c].astype(F32),
        )

    def x_update(c):
        half = pl.ds(0, HB)
        arrived(r2_v.at[c, 0, 0, half], r_raw.at[c, 0])
        arrived(r2_v.at[c, 1, 0, half], r_raw.at[c, 1])
        arrived(r2_v.at[c, 0, 0, half], r_acc.at[c, 0])
        arrived(r2_v.at[c, 1, 0, half], r_acc.at[c, 1])
        update(
            c,
            inner_v[c, xh, 0].astype(F32)
            + rxx_v[c // X_EVERY, 0].astype(F32)
            + r2_v[c, 0, 0].astype(F32)
            + r2_v[c, 1, 0].astype(F32),
        )

    def z_partner(c):
        theirs = block_of(c, 1 - xh, z)
        arrived(theirs, r_gx.at[c])
        remote(theirs, theirs, c, r_gp.at[c, 0], to_up).start()
        remote(theirs, theirs, c, r_gp.at[c, 1], to_dn).start()

    def z_forward(c):
        arrived(block_of(c, xh, dn_z), r_go.at[c, 0])
        arrived(block_of(c, 1 - xh, dn_z), r_gp.at[c, 0])
        low = block_of(c, 0, dn_z)
        remote(low, low, c, r_gf.at[c, 0], to_up).start()
        arrived(block_of(c, xh, up_z), r_go.at[c, 1])
        arrived(block_of(c, 1 - xh, up_z), r_gp.at[c, 1])
        high = block_of(c, 1, up_z)
        remote(high, high, c, r_gf.at[c, 1], to_dn).start()

    def z_last(c):
        arrived(block_of(c, 0, op_z), r_gf.at[c, 0])
        arrived(block_of(c, 1, op_z), r_gf.at[c, 1])

    def half_of(c, half, zz, part):
        return nw_out.at[half * N_Z + zz, pl.ds(part * HB, HB), cols(c)]

    def x_neighbours(c):
        below = block_of(c, xh, dn_z)
        arrived(below, r_go.at[c, 0])
        part = half_of(c, xh, dn_z, 0)
        remote(part, part, c, r_gf.at[c, 0], to_up).start()
        remote(below, below, c, r_gp.at[c, 0], to_x).start()
        above = block_of(c, xh, up_z)
        arrived(above, r_go.at[c, 1])
        part = half_of(c, xh, up_z, 1)
        remote(part, part, c, r_gf.at[c, 1], to_dn).start()
        remote(above, above, c, r_gp.at[c, 1], to_x).start()

    def x_far(c):
        arrived(half_of(c, xh, op_z, 0), r_gf.at[c, 0])
        arrived(half_of(c, xh, op_z, 1), r_gf.at[c, 1])
        far = block_of(c, xh, op_z)
        remote(far, far, c, r_gz.at[c], to_x).start()

    def x_last(c):
        arrived(block_of(c, 1 - xh, z), r_gx.at[c])
        arrived(block_of(c, 1 - xh, dn_z), r_gp.at[c, 0])
        arrived(block_of(c, 1 - xh, up_z), r_gp.at[c, 1])
        arrived(block_of(c, 1 - xh, op_z), r_gz.at[c])

    def either(z_step, x_step):
        def step(c):
            is_x = lax.rem(c, X_EVERY) == X_AT

            @pl.when(is_x)
            def _():
                x_step(c)

            @pl.when(jnp.logical_not(is_x))
            def _():
                z_step(c)

        return step

    def up_form(c):
        w_all = w_v[c].reshape(N_ISL * RB, W)
        lhs = x_v[1 - core].reshape(PLANE * TB, N_ISL * RB)
        ups_v[c] = jnp.dot(lhs, w_all, preferred_element_type=F32).astype(BF16)
        remote(ups_v.at[c], upr_v.at[c], c, r_ups.at[c], to_sib).start()
        lhs = x_v[core].reshape(PLANE * TB, N_ISL * RB)
        upo_v[c] = jnp.dot(lhs, w_all, preferred_element_type=F32).astype(BF16)

    def up_add(c):
        arrived(upr_v.at[c], r_ups.at[c])
        both = upo_v[c].astype(F32) + upr_v[c].astype(F32)
        upt_v[pl.ds(c * PLANE, PLANE)] = both.astype(BF16).reshape(PLANE, TB, W)
        for k in range(1, PLANE):
            to = lax.rem(place + k, PLANE)
            remote(
                upt_v.at[c * PLANE + to], upp_v.at[c * PLANE + place], c, r_upp.at[c], peer(k)
            ).start()

    def up_last(c):
        arrived(upp_v.at[pl.ds(c * PLANE, PLANE - 1)], r_upp.at[c])
        up = upt_v[c * PLANE + place].astype(F32)
        for k in range(1, PLANE):
            up = up + upp_v[c * PLANE + lax.rem(place + k, PLANE)].astype(F32)
        g = gate_v[:, cols(c)].astype(F32)
        s = jax.nn.sigmoid(g)
        out = cot_v[:, cols(c)].astype(F32) * up * s * (1.0 + g * (1.0 - s))
        gg_out[:, cols(c)] = out.astype(BF16)

    def ig_form(c):
        d_up = dup_v[pl.ds(c * 16, 16)].reshape(16 * TB, W)
        w_all = w_v[c].reshape(N_ISL * RB, W)
        part = lax.dot_general(
            d_up, w_all, (((1,), (1,)), ((), ())), preferred_element_type=F32
        )
        acc_v[...] += part

    in_copies[0].wait()
    in_copies[1].wait()
    w_copy(0).start()
    dup_form(0)
    pl.semaphore_wait(barrier, 3 + PLANE)
    dup_send(0)

    @pl.loop(1, 3)
    def _(c):
        dup_form(c)
        dup_send(c)

    @pl.loop(1, n_chunk)
    def _(c):
        w_copy(c).start()

    in_copies[4].start()
    in_copies[5].start()
    in_copies[2].wait()
    in_copies[3].wait()
    for block in range(N_ISL):
        piece = x_v[:, :, :, block * RB : (block + 1) * RB].reshape(16 * TB, RB)
        rel = lax.rem(block % N_Z + N_Z - z, N_Z)
        xt_v[block // N_Z, rel] = piece.T
    acc_v[...] = jnp.zeros_like(acc_v)
    dup_share(0)

    def at(c, lo, hi, *steps):
        @pl.when((c >= lo) & (c < hi))
        def _():
            for step in steps:
                step(c)

    @pl.loop(0, n_chunk + LAG_F)
    def _(t):
        def ahead(c):
            dup_form(c)
            dup_send(c)

        at(t + 3, 0, n_chunk, ahead)
        at(t + 1, 0, n_chunk, dup_share)

        def start_sum(c):
            w_copy(c).wait()
            inner_form(c)
            either(z_first, x_first)(c)
            up_form(c)

        at(t, 0, n_chunk, start_sum)
        at(t - LAG_A, 0, n_chunk, either(z_second, x_second))
        at(t - LAG_B, 0, n_chunk, either(z_third, x_third))

        @pl.when(t == LAG_C)
        def _():
            in_copies[4].wait()
            in_copies[5].wait()

        at(t - LAG_C, 0, n_chunk, either(z_update, x_update))
        at(t - LAG_D, 0, n_chunk, either(z_partner, x_neighbours))
        at(t - LAG_E, 0, n_chunk, either(z_forward, x_far))
        at(t, 0, n_chunk, ig_form)
        at(t - LAG_UA, 0, n_chunk, up_add)
        at(t - LAG_UB, 0, n_chunk, up_last)
        at(t - LAG_F, 0, n_chunk, either(z_last, x_last))

    for half in range(2):
        ig_out[:, half] = acc_v[half * PLANE * TB : (half + 1) * PLANE * TB].astype(BF16).reshape(
            PLANE, TB, N_ISL * RB
        )

    sent = (2 * 7 * TB + 2 * PLANE * TB + 6 * RB + RB + 3 * RB + 2 * RB + 2 * RB) // TB

    @pl.loop(0, n_chunk)
    def _(c):
        arrived(dup_v.at[pl.ds(0, sent)], snd.at[c])


def local(inputs, gate_pre, up_cot, weights, outer, momentum):
    d_loc, fs = weights.shape[1], weights.shape[2]
    tok = inputs.shape[1]
    c = fs // W
    dma = pltpu.SemaphoreType.DMA
    vmem = pl.BlockSpec(memory_space=pltpu.VMEM)
    hbm = pl.BlockSpec(memory_space=pltpu.HBM)
    ig, gg, nw, no, nm = pl.pallas_call(
        functools.partial(kernel, c),
        out_shape=(
            pltpu.VMEM((PLANE, 2, TB, d_loc), BF16),
            pltpu.VMEM((TB, fs), BF16),
            pltpu.VMEM((N_ISL, RB, fs), BF16),
            pltpu.VMEM((RB, fs), F32),
            pltpu.VMEM((RB, fs), F32),
        ),
        in_specs=[hbm] * 6,
        out_specs=(vmem,) * 5,
        scratch_shapes=[
            pltpu.VMEM((2, PLANE, TB, d_loc), BF16),
            pltpu.VMEM((2, N_Z, RB, tok), BF16),
            pltpu.VMEM((TB, fs), BF16),
            pltpu.VMEM((TB, fs), BF16),
            pltpu.VMEM((RB, fs), F32),
            pltpu.VMEM((RB, fs), F32),
            pltpu.VMEM((c, N_ISL, RB, W), BF16),
            pltpu.VMEM((c * 16, TB, W), BF16),
            pltpu.VMEM((c, 2, N_Z, RB, W), BF16),
            pltpu.VMEM((c, 2, RB, W), BF16),
            pltpu.VMEM((c, 2, 2, RB, W), BF16),
            pltpu.VMEM((c, RB, W), BF16),
            pltpu.VMEM((c, RB, W), BF16),
            pltpu.VMEM((-(-c // X_EVERY), N_Z, RB, W), BF16),
            pltpu.VMEM((c, PLANE * TB, W), BF16),
            pltpu.VMEM((c, PLANE * TB, W), BF16),
            pltpu.VMEM((c, PLANE * TB, W), BF16),
            pltpu.VMEM((c * PLANE, TB, W), BF16),
            pltpu.VMEM((c * PLANE, TB, W), BF16),
            pltpu.VMEM((tok, d_loc), F32),
            dma((6,)),
            dma((c,)),
            dma((c,)),
            dma((c,)),
            dma((c,)),
            dma((c, 2)),
            dma((c, 2)),
            dma((c, 2)),
            dma((c,)),
            dma((c,)),
            dma((c, 2)),
            dma((c, 2)),
            dma((c, 2)),
            dma((c,)),
            dma((c,)),
            dma((c,)),
        ],
        compiler_params=pltpu.CompilerParams(
            collective_id=0, has_side_effects=True, vmem_limit_bytes=48 * 2**20
        ),
        cost_estimate=pl.CostEstimate(
            flops=6 * tok * d_loc * fs, bytes_accessed=8 * d_loc * fs, transcendentals=0
        ),
    )(
        inputs.reshape(PLANE, 2, TB, d_loc),
        gate_pre[0],
        up_cot[0],
        weights.reshape(N_ISL, RB, fs),
        outer,
        momentum,
    )
    return (
        ig.reshape(1, tok, d_loc),
        gg[None],
        nw.reshape(d_loc, fs),
        no,
        nm,
    )


def solution(mesh):
    placed = (
        P("island", None, "section"),
        P("island", "section", None),
        P("island", "section", None),
        P("island", "section", None),
        P(("section", "island"), None),
        P(("section", "island"), None),
    )
    return jax.shard_map(
        local,
        mesh=mesh,
        in_specs=placed,
        out_specs=(
            P("island", None, "section"),
            P("island", "section", None),
            P("section", None),
            P(("section", "island"), None),
            P(("section", "island"), None),
        ),
        check_vma=False,
    )
```

```python
import functools

import jax
import jax.numpy as jnp
from jax import lax
from jax.experimental import pallas as pl
from jax.experimental.pallas import tpu as pltpu
from jax.sharding import PartitionSpec as P

inner_rate = 0.0005
outer_rate = 0.7
nesterov_mu = 0.9

MESH = pl.DeviceIdType.MESH
F32 = jnp.float32
BF16 = jnp.bfloat16

W = 256
N_Z = 4
N_ISL = 8
N_Y = 4
PLANE = 8
TB = 32
RB = 128
HB = RB // 2
X_CHUNKS = (0, 4, 6, 9, 11)
LAG_A, LAG_B, LAG_C, LAG_D, LAG_E, LAG_F = 2, 4, 6, 10, 14, 18
LAG_UA, LAG_UB, LAG_UC = 6, 9, 14
AHEAD_B, AHEAD_C = 2, 1


def kernel(
    n_chunk,
    x_hbm, gate_hbm, cot_hbm, w_hbm, outer_hbm, mom_hbm,
    ig_out, gg_out, nw_out, no_out, nm_out,
    x_v, xt_v, gate_v, cot_v, outer_v, mom_v, w_v, dup_v,
    inner_v, r1_v, r2_v, xs_v, rx_v, rxx_v,
    ups_v, upr_v, upo_v, upt_v, upp_v, upx_v, upy_v, acc_v,
    in_sem, w_sem, snd, r_dup, r_dx, r_sib, r_s1, r_raw, r_acc, r_x,
    r_gx, r_go, r_gp, r_gf, r_gz, r_ups, r_upp, r_upx,
):
    sec = lax.axis_index("section")
    isl = lax.axis_index("island")
    core = lax.rem(sec, 2)
    place = sec // 2
    xl = place // N_Y
    y = lax.rem(place, N_Y)
    z = lax.rem(isl, N_Z)
    xh = isl // N_Z
    up_z = lax.rem(z + 1, N_Z)
    dn_z = lax.rem(z + N_Z - 1, N_Z)
    op_z = lax.rem(z + 2, N_Z)
    to_up = (sec, xh * N_Z + up_z)
    to_dn = (sec, xh * N_Z + dn_z)
    to_x = (sec, (1 - xh) * N_Z + z)
    to_sib = (place * 2 + 1 - core, isl)

    to_xl = (((1 - xl) * N_Y + y) * 2 + core, isl)

    def along_y(k):
        return lax.rem(y + k, N_Y)

    def peer(x_at, y_at):
        return ((x_at * N_Y + y_at) * 2 + core, isl)

    def remote(src, dst, c, recv, device):
        return pltpu.make_async_remote_copy(
            src_ref=src, dst_ref=dst, send_sem=snd.at[c], recv_sem=recv,
            device_id=device, device_id_type=MESH,
        )

    def arrived(dst, recv):
        pltpu.make_async_copy(dst, dst, recv).wait()

    def x_slot(c):
        return sum((c > k).astype(jnp.int32) for k in X_CHUNKS)

    def cols(c):
        return pl.ds(pl.multiple_of(c * W, W), W)

    barrier = pltpu.get_barrier_semaphore()
    others = [(xl, along_y(k)) for k in (1, 2, 3)]
    others += [(1 - xl, along_y(k)) for k in (0, 1, 2, 3)]
    for device in [peer(*other) for other in others] + [to_sib, to_up, to_dn, to_x]:
        pl.semaphore_signal(barrier, inc=1, device_id=device, device_id_type=MESH)

    def w_copy(c):
        return pltpu.make_async_copy(w_hbm.at[:, :, cols(c)], w_v.at[c], w_sem.at[c])

    in_copies = [
        pltpu.make_async_copy(gate_hbm, gate_v, in_sem.at[0]),
        pltpu.make_async_copy(cot_hbm, cot_v, in_sem.at[1]),
        pltpu.make_async_copy(x_hbm.at[:, 0], x_v.at[0], in_sem.at[2]),
        pltpu.make_async_copy(x_hbm.at[:, 1], x_v.at[1], in_sem.at[3]),
        pltpu.make_async_copy(outer_hbm, outer_v, in_sem.at[4]),
        pltpu.make_async_copy(mom_hbm, mom_v, in_sem.at[5]),
    ]
    for copy in in_copies[:4]:
        copy.start()

    def dup_form(c):
        g = gate_v[:, cols(c)].astype(F32)
        s = jax.nn.sigmoid(g)
        d = cot_v[:, cols(c)].astype(F32) * g * s
        dup_v[c * 16 + core * PLANE + place] = d.astype(BF16)

    def dup_at(c, p):
        return dup_v.at[c * 16 + core * PLANE + p]

    def dup_send_all(c):
        mine = dup_at(c, place)
        for other in others:
            recv = r_dx.at[c] if other is others[3] else r_dup.at[c]
            remote(mine, mine, c, recv, peer(*other)).start()

    def dup_send(c):
        mine = dup_at(c, place)
        remote(mine, mine, c, r_dx.at[c], to_xl).start()
        for other in others[:3]:
            remote(mine, mine, c, r_dup.at[c], peer(*other)).start()

    def dup_pass(c):
        theirs = dup_at(c, (1 - xl) * N_Y + y)
        arrived(theirs, r_dx.at[c])
        for other in others[:3]:
            remote(theirs, theirs, c, r_dup.at[c], peer(*other)).start()

    def dup_share(c):
        arrived(dup_v.at[pl.ds(c * 16 + core * PLANE, PLANE - 2)], r_dup.at[c])
        half = dup_v.at[pl.ds(c * 16 + core * PLANE, PLANE)]
        remote(half, half, c, r_sib.at[c], to_sib).start()

    def inner_form(c):
        arrived(dup_v.at[pl.ds(c * 16 + (1 - core) * PLANE, PLANE)], r_sib.at[c])
        d_up = dup_v[pl.ds(c * 16, 16)].reshape(16 * TB, W)
        for half in (1 - xh, xh):
            lhs = xt_v[half].reshape(N_Z * RB, 16 * TB)
            grad = jnp.dot(lhs, d_up, preferred_element_type=F32)
            for rel in range(N_Z):
                block = half * N_Z + lax.rem(z + rel, N_Z)
                w_part = w_v[c, block].astype(F32)
                inner_v[c, half, rel] = (
                    w_part - inner_rate * grad[rel * RB : (rel + 1) * RB]
                ).astype(BF16)

    def add_into(dst, other):
        dst[...] = (dst[...].astype(F32) + other[...].astype(F32)).astype(BF16)

    def z_first(c):
        remote(inner_v.at[c, 0, 2], r1_v.at[c, 0], c, r_s1.at[c, 0], to_up).start()
        remote(inner_v.at[c, 1, 2], r1_v.at[c, 1], c, r_s1.at[c, 1], to_dn).start()
        remote(inner_v.at[c, 1, 1], r2_v.at[c, 0, 1], c, r_raw.at[c, 0], to_up).start()
        remote(inner_v.at[c, 0, 3], r2_v.at[c, 1, 0], c, r_raw.at[c, 1], to_dn).start()

    def z_second(c):
        arrived(r1_v.at[c, 0], r_s1.at[c, 0])
        add_into(inner_v.at[c, 0, 1], r1_v.at[c, 0])
        remote(inner_v.at[c, 0, 1], r2_v.at[c, 0, 0], c, r_acc.at[c, 0], to_up).start()
        arrived(r1_v.at[c, 1], r_s1.at[c, 1])
        add_into(inner_v.at[c, 1, 3], r1_v.at[c, 1])
        remote(inner_v.at[c, 1, 3], r2_v.at[c, 1, 1], c, r_acc.at[c, 1], to_dn).start()

    def z_third(c):
        arrived(r2_v.at[c, 0, 1], r_raw.at[c, 0])
        arrived(r2_v.at[c, 1, 0], r_raw.at[c, 1])
        arrived(r2_v.at[c, 0, 0], r_acc.at[c, 0])
        arrived(r2_v.at[c, 1, 1], r_acc.at[c, 1])
        xs_v[c] = (
            inner_v[c, 1 - xh, 0].astype(F32)
            + r2_v[c, 0, 1 - xh].astype(F32)
            + r2_v[c, 1, 1 - xh].astype(F32)
        ).astype(BF16)
        remote(xs_v.at[c], rx_v.at[c], c, r_x.at[c], to_x).start()

    def x_first(c):
        remote(inner_v.at[c, 1 - xh], rxx_v.at[x_slot(c)], c, r_x.at[c], to_x).start()

    def x_second(c):
        got = rxx_v.at[x_slot(c)]
        arrived(got, r_x.at[c])
        low, high = pl.ds(0, HB), pl.ds(HB, HB)
        far, above, below = (inner_v.at[c, xh, rel] for rel in (2, 1, 3))
        add_into(far, got.at[2])
        remote(far.at[low], r1_v.at[c, 0, low], c, r_s1.at[c, 0], to_up).start()
        remote(far.at[high], r1_v.at[c, 1, low], c, r_s1.at[c, 1], to_dn).start()
        add_into(above, got.at[1])
        remote(above.at[high], r2_v.at[c, 0, 0, high], c, r_raw.at[c, 0], to_up).start()
        add_into(below, got.at[3])
        remote(below.at[low], r2_v.at[c, 1, 0, low], c, r_raw.at[c, 1], to_dn).start()

    def x_third(c):
        low, high = pl.ds(0, HB), pl.ds(HB, HB)
        arrived(r1_v.at[c, 0, low], r_s1.at[c, 0])
        above = inner_v.at[c, xh, 1, low]
        add_into(above, r1_v.at[c, 0, low])
        remote(above, r2_v.at[c, 0, 0, low], c, r_acc.at[c, 0], to_up).start()
        arrived(r1_v.at[c, 1, low], r_s1.at[c, 1])
        below = inner_v.at[c, xh, 3, high]
        add_into(below, r1_v.at[c, 1, low])
        remote(below, r2_v.at[c, 1, 0, high], c, r_acc.at[c, 1], to_dn).start()

    def block_of(c, half, zz):
        return nw_out.at[half * N_Z + zz, :, cols(c)]

    def update(c, total):
        own = outer_v[:, cols(c)]
        delta = own - total * (1.0 / N_ISL)
        moment = nesterov_mu * mom_v[:, cols(c)] + delta
        new = own - outer_rate * (delta + nesterov_mu * moment)
        nm_out[:, cols(c)] = moment
        no_out[:, cols(c)] = new
        nw_out[isl, :, cols(c)] = new.astype(BF16)
        mine = block_of(c, xh, z)
        remote(mine, mine, c, r_gx.at[c], to_x).start()
        remote(mine, mine, c, r_go.at[c, 0], to_up).start()
        remote(mine, mine, c, r_go.at[c, 1], to_dn).start()

    def z_update(c):
        arrived(rx_v.at[c], r_x.at[c])
        update(
            c,
            inner_v[c, xh, 0].astype(F32)
            + r2_v[c, 0, xh].astype(F32)
            + r2_v[c, 1, xh].astype(F32)
            + rx_v[c].astype(F32),
        )

    def x_update(c):
        half = pl.ds(0, HB)
        arrived(r2_v.at[c, 0, 0, half], r_raw.at[c, 0])
        arrived(r2_v.at[c, 1, 0, half], r_raw.at[c, 1])
        arrived(r2_v.at[c, 0, 0, half], r_acc.at[c, 0])
        arrived(r2_v.at[c, 1, 0, half], r_acc.at[c, 1])
        update(
            c,
            inner_v[c, xh, 0].astype(F32)
            + rxx_v[x_slot(c), 0].astype(F32)
            + r2_v[c, 0, 0].astype(F32)
            + r2_v[c, 1, 0].astype(F32),
        )

    def z_partner(c):
        theirs = block_of(c, 1 - xh, z)
        arrived(theirs, r_gx.at[c])
        remote(theirs, theirs, c, r_gp.at[c, 0], to_up).start()
        remote(theirs, theirs, c, r_gp.at[c, 1], to_dn).start()

    def z_forward(c):
        arrived(block_of(c, xh, dn_z), r_go.at[c, 0])
        arrived(block_of(c, 1 - xh, dn_z), r_gp.at[c, 0])
        low = block_of(c, 0, dn_z)
        remote(low, low, c, r_gf.at[c, 0], to_up).start()
        arrived(block_of(c, xh, up_z), r_go.at[c, 1])
        arrived(block_of(c, 1 - xh, up_z), r_gp.at[c, 1])
        high = block_of(c, 1, up_z)
        remote(high, high, c, r_gf.at[c, 1], to_dn).start()

    def z_last(c):
        arrived(block_of(c, 0, op_z), r_gf.at[c, 0])
        arrived(block_of(c, 1, op_z), r_gf.at[c, 1])

    def half_of(c, half, zz, part):
        return nw_out.at[half * N_Z + zz, pl.ds(part * HB, HB), cols(c)]

    def x_neighbours(c):
        below = block_of(c, xh, dn_z)
        arrived(below, r_go.at[c, 0])
        part = half_of(c, xh, dn_z, 0)
        remote(part, part, c, r_gf.at[c, 0], to_up).start()
        remote(below, below, c, r_gp.at[c, 0], to_x).start()
        above = block_of(c, xh, up_z)
        arrived(above, r_go.at[c, 1])
        part = half_of(c, xh, up_z, 1)
        remote(part, part, c, r_gf.at[c, 1], to_dn).start()
        remote(above, above, c, r_gp.at[c, 1], to_x).start()

    def x_far(c):
        arrived(half_of(c, xh, op_z, 0), r_gf.at[c, 0])
        arrived(half_of(c, xh, op_z, 1), r_gf.at[c, 1])
        far = block_of(c, xh, op_z)
        remote(far, far, c, r_gz.at[c], to_x).start()

    def x_last(c):
        arrived(block_of(c, 1 - xh, z), r_gx.at[c])
        arrived(block_of(c, 1 - xh, dn_z), r_gp.at[c, 0])
        arrived(block_of(c, 1 - xh, up_z), r_gp.at[c, 1])
        arrived(block_of(c, 1 - xh, op_z), r_gz.at[c])

    def either(z_step, x_step):
        def step(c):
            is_x = functools.reduce(jnp.logical_or, [c == k for k in X_CHUNKS])

            @pl.when(is_x)
            def _():
                x_step(c)

            @pl.when(jnp.logical_not(is_x))
            def _():
                z_step(c)

        return step

    def up_form(c):
        w_all = w_v[c].reshape(N_ISL * RB, W)
        lhs = x_v[1 - core].reshape(PLANE * TB, N_ISL * RB)
        ups_v[c] = jnp.dot(lhs, w_all, preferred_element_type=F32).astype(BF16)
        remote(ups_v.at[c], upr_v.at[c], c, r_ups.at[c], to_sib).start()
        lhs = x_v[core].reshape(PLANE * TB, N_ISL * RB)
        upo_v[c] = jnp.dot(lhs, w_all, preferred_element_type=F32).astype(BF16)

    def up_add(c):
        arrived(upr_v.at[c], r_ups.at[c])
        both = upo_v[c].astype(F32) + upr_v[c].astype(F32)
        upt_v[c] = both.astype(BF16).reshape(2, N_Y, TB, W)
        for k in (1, 2, 3):
            to = along_y(k)
            remote(
                upt_v.at[c, :, to], upp_v.at[c, y], c, r_upp.at[c], peer(xl, to)
            ).start()

    def up_cross(c):
        arrived(upp_v.at[c, pl.ds(0, N_Y - 1)], r_upp.at[c])
        total = upt_v[c, :, y].astype(F32)
        for k in (1, 2, 3):
            total = total + upp_v[c, along_y(k)].astype(F32)
        upy_v[c] = total.astype(BF16)
        remote(upy_v.at[c, 1 - xl], upx_v.at[c], c, r_upx.at[c], to_xl).start()

    def up_last(c):
        arrived(upx_v.at[c], r_upx.at[c])
        up = upy_v[c, xl].astype(F32) + upx_v[c].astype(F32)
        g = gate_v[:, cols(c)].astype(F32)
        s = jax.nn.sigmoid(g)
        out = cot_v[:, cols(c)].astype(F32) * up * s * (1.0 + g * (1.0 - s))
        gg_out[:, cols(c)] = out.astype(BF16)

    def ig_form(c):
        d_up = dup_v[pl.ds(c * 16, 16)].reshape(16 * TB, W)
        w_all = w_v[c].reshape(N_ISL * RB, W)
        part = lax.dot_general(
            d_up, w_all, (((1,), (1,)), ((), ())), preferred_element_type=F32
        )
        acc_v[...] += part

    in_copies[0].wait()
    in_copies[1].wait()
    @pl.loop(0, n_chunk)
    def _(c):
        dup_form(c)

    pl.semaphore_wait(barrier, 4 + PLANE - 1)
    dup_send_all(0)

    @pl.loop(1, n_chunk)
    def _(c):
        dup_send(c)

    w_copy(0).start()
    in_copies[2].wait()
    in_copies[3].wait()
    for block in range(N_ISL):
        piece = x_v[:, :, :, block * RB : (block + 1) * RB].reshape(16 * TB, RB)
        rel = lax.rem(block % N_Z + N_Z - z, N_Z)
        xt_v[block // N_Z, rel] = piece.T
    arrived(dup_at(0, (1 - xl) * N_Y + y), r_dx.at[0])
    dup_share(0)

    @pl.loop(1, n_chunk)
    def _(c):
        w_copy(c).start()

    @pl.loop(1, AHEAD_B)
    def _(c):
        dup_pass(c)

    in_copies[4].start()
    in_copies[5].start()
    acc_v[...] = jnp.zeros_like(acc_v)

    def at(c, lo, hi, *steps):
        @pl.when((c >= lo) & (c < hi))
        def _():
            for step in steps:
                step(c)

    @pl.loop(0, n_chunk + LAG_F)
    def _(t):
        def start_sum(c):
            w_copy(c).wait()
            inner_form(c)
            either(z_first, x_first)(c)
            up_form(c)

        at(t, 0, n_chunk, start_sum)

        at(t + AHEAD_B, 0, n_chunk, dup_pass)
        at(t + AHEAD_C, 0, n_chunk, dup_share)
        at(t - LAG_A, 0, n_chunk, either(z_second, x_second))
        at(t - LAG_B, 0, n_chunk, either(z_third, x_third))

        @pl.when(t == LAG_C)
        def _():
            in_copies[4].wait()
            in_copies[5].wait()

        at(t - LAG_C, 0, n_chunk, either(z_update, x_update))
        at(t - LAG_D, 0, n_chunk, either(z_partner, x_neighbours))
        at(t - LAG_E, 0, n_chunk, either(z_forward, x_far))
        at(t, 0, n_chunk, ig_form)

        @pl.when(t == n_chunk + LAG_A)
        def _():
            for half in range(2):
                rows = acc_v[half * PLANE * TB : (half + 1) * PLANE * TB].astype(BF16)
                ig_out[:, half] = rows.reshape(PLANE, TB, N_ISL * RB)

        at(t - LAG_UA, 0, n_chunk, up_add)
        at(t - LAG_UB, 0, n_chunk, up_cross)
        at(t - LAG_UC, 0, n_chunk, up_last)
        at(t - LAG_F, 0, n_chunk, either(z_last, x_last))

    sent = (2 * 7 * TB + 2 * PLANE * TB + 6 * RB + RB + 3 * RB + 2 * RB + 2 * RB) // TB

    @pl.loop(0, n_chunk)
    def _(c):
        arrived(dup_v.at[pl.ds(0, sent)], snd.at[c])


def local(inputs, gate_pre, up_cot, weights, outer, momentum):
    d_loc, fs = weights.shape[1], weights.shape[2]
    tok = inputs.shape[1]
    c = fs // W
    dma = pltpu.SemaphoreType.DMA
    vmem = pl.BlockSpec(memory_space=pltpu.VMEM)
    hbm = pl.BlockSpec(memory_space=pltpu.HBM)
    ig, gg, nw, no, nm = pl.pallas_call(
        functools.partial(kernel, c),
        out_shape=(
            pltpu.VMEM((PLANE, 2, TB, d_loc), BF16),
            pltpu.VMEM((TB, fs), BF16),
            pltpu.VMEM((N_ISL, RB, fs), BF16),
            pltpu.VMEM((RB, fs), F32),
            pltpu.VMEM((RB, fs), F32),
        ),
        in_specs=[hbm] * 6,
        out_specs=(vmem,) * 5,
        scratch_shapes=[
            pltpu.VMEM((2, PLANE, TB, d_loc), BF16),
            pltpu.VMEM((2, N_Z, RB, tok), BF16),
            pltpu.VMEM((TB, fs), BF16),
            pltpu.VMEM((TB, fs), BF16),
            pltpu.VMEM((RB, fs), F32),
            pltpu.VMEM((RB, fs), F32),
            pltpu.VMEM((c, N_ISL, RB, W), BF16),
            pltpu.VMEM((c * 16, TB, W), BF16),
            pltpu.VMEM((c, 2, N_Z, RB, W), BF16),
            pltpu.VMEM((c, 2, RB, W), BF16),
            pltpu.VMEM((c, 2, 2, RB, W), BF16),
            pltpu.VMEM((c, RB, W), BF16),
            pltpu.VMEM((c, RB, W), BF16),
            pltpu.VMEM((len(X_CHUNKS), N_Z, RB, W), BF16),
            pltpu.VMEM((c, PLANE * TB, W), BF16),
            pltpu.VMEM((c, PLANE * TB, W), BF16),
            pltpu.VMEM((c, PLANE * TB, W), BF16),
            pltpu.VMEM((c, 2, N_Y, TB, W), BF16),
            pltpu.VMEM((c, N_Y, 2, TB, W), BF16),
            pltpu.VMEM((c, TB, W), BF16),
            pltpu.VMEM((c, 2, TB, W), BF16),
            pltpu.VMEM((tok, d_loc), F32),
            dma((6,)),
            dma((c,)),
            dma((c,)),
            dma((c,)),
            dma((c,)),
            dma((c,)),
            dma((c, 2)),
            dma((c, 2)),
            dma((c, 2)),
            dma((c,)),
            dma((c,)),
            dma((c, 2)),
            dma((c, 2)),
            dma((c, 2)),
            dma((c,)),
            dma((c,)),
            dma((c,)),
            dma((c,)),
        ],
        compiler_params=pltpu.CompilerParams(
            collective_id=0, has_side_effects=True, vmem_limit_bytes=48 * 2**20
        ),
        cost_estimate=pl.CostEstimate(
            flops=6 * tok * d_loc * fs, bytes_accessed=8 * d_loc * fs, transcendentals=0
        ),
    )(
        inputs.reshape(PLANE, 2, TB, d_loc),
        gate_pre[0],
        up_cot[0],
        weights.reshape(N_ISL, RB, fs),
        outer,
        momentum,
    )
    return (
        ig.reshape(1, tok, d_loc),
        gg[None],
        nw.reshape(d_loc, fs),
        no,
        nm,
    )


def solution(mesh):
    placed = (
        P("island", None, "section"),
        P("island", "section", None),
        P("island", "section", None),
        P("island", "section", None),
        P(("section", "island"), None),
        P(("section", "island"), None),
    )
    return jax.shard_map(
        local,
        mesh=mesh,
        in_specs=placed,
        out_specs=(
            P("island", None, "section"),
            P("island", "section", None),
            P("section", None),
            P(("section", "island"), None),
            P(("section", "island"), None),
        ),
        check_vma=False,
    )
```

```python
import functools

import jax
import jax.numpy as jnp
from jax import lax
from jax.experimental import pallas as pl
from jax.experimental.pallas import tpu as pltpu
from jax.sharding import PartitionSpec as P

inner_rate = 0.0005
outer_rate = 0.7
nesterov_mu = 0.9

MESH = pl.DeviceIdType.MESH
F32 = jnp.float32
BF16 = jnp.bfloat16

W = 256
N_Z = 4
N_ISL = 8
N_Y = 4
PLANE = 8
TB = 32
RB = 128
HB = RB // 2
X_CHUNKS = (0, 4, 6, 9, 11)
LAG_A, LAG_B, LAG_C, LAG_D, LAG_E, LAG_F = 2, 4, 6, 10, 14, 18
LAG_UA, LAG_UB, LAG_UC = 6, 9, 14
AHEAD_B, AHEAD_C = 2, 1
FIRST = 3


def kernel(
    n_chunk,
    x_hbm, gate_hbm, cot_hbm, w_hbm, outer_hbm, mom_hbm,
    ig_out, gg_out, nw_out, no_out, nm_out,
    x_v, xt_v, gate_v, cot_v, outer_v, mom_v, w_v, dup_v,
    inner_v, r1_v, r2_v, xs_v, rx_v, rxx_v,
    ups_v, upr_v, upo_v, upt_v, upp_v, upx_v, upy_v, acc_v,
    in_sem, w_sem, snd, r_dup, r_dx, r_sib, r_s1, r_raw, r_acc, r_x,
    r_gx, r_go, r_gp, r_gf, r_gz, r_ups, r_upp, r_upx,
):
    sec = lax.axis_index("section")
    isl = lax.axis_index("island")
    core = lax.rem(sec, 2)
    place = sec // 2
    xl = place // N_Y
    y = lax.rem(place, N_Y)
    z = lax.rem(isl, N_Z)
    xh = isl // N_Z
    up_z = lax.rem(z + 1, N_Z)
    dn_z = lax.rem(z + N_Z - 1, N_Z)
    op_z = lax.rem(z + 2, N_Z)
    to_up = (sec, xh * N_Z + up_z)
    to_dn = (sec, xh * N_Z + dn_z)
    to_x = (sec, (1 - xh) * N_Z + z)
    to_sib = (place * 2 + 1 - core, isl)

    to_xl = (((1 - xl) * N_Y + y) * 2 + core, isl)

    def along_y(k):
        return lax.rem(y + k, N_Y)

    def peer(x_at, y_at):
        return ((x_at * N_Y + y_at) * 2 + core, isl)

    def remote(src, dst, c, recv, device):
        return pltpu.make_async_remote_copy(
            src_ref=src, dst_ref=dst, send_sem=snd.at[c], recv_sem=recv,
            device_id=device, device_id_type=MESH,
        )

    def arrived(dst, recv):
        pltpu.make_async_copy(dst, dst, recv).wait()

    def x_slot(c):
        return sum((c > k).astype(jnp.int32) for k in X_CHUNKS)

    def cols(c):
        return pl.ds(pl.multiple_of(c * W, W), W)

    barrier = pltpu.get_barrier_semaphore()
    others = [(xl, along_y(k)) for k in (1, 2, 3)]
    others += [(1 - xl, along_y(k)) for k in (0, 1, 2, 3)]
    for device in [peer(*other) for other in others] + [to_sib, to_up, to_dn, to_x]:
        pl.semaphore_signal(barrier, inc=1, device_id=device, device_id_type=MESH)

    def w_copy(c):
        return pltpu.make_async_copy(w_hbm.at[:, :, cols(c)], w_v.at[c], w_sem.at[c])

    in_copies = [
        pltpu.make_async_copy(gate_hbm, gate_v, in_sem.at[0]),
        pltpu.make_async_copy(cot_hbm, cot_v, in_sem.at[1]),
        pltpu.make_async_copy(x_hbm.at[:, 0], x_v.at[0], in_sem.at[2]),
        pltpu.make_async_copy(x_hbm.at[:, 1], x_v.at[1], in_sem.at[3]),
        pltpu.make_async_copy(outer_hbm, outer_v, in_sem.at[4]),
        pltpu.make_async_copy(mom_hbm, mom_v, in_sem.at[5]),
    ]
    for copy in in_copies[:4]:
        copy.start()

    def dup_form(c):
        g = gate_v[:, cols(c)].astype(F32)
        s = jax.nn.sigmoid(g)
        d = cot_v[:, cols(c)].astype(F32) * g * s
        dup_v[c * 16 + core * PLANE + place] = d.astype(BF16)

    def dup_at(c, p):
        return dup_v.at[c * 16 + core * PLANE + p]

    def dup_send_all(c):
        mine = dup_at(c, place)
        for other in others:
            recv = r_dx.at[c] if other is others[3] else r_dup.at[c]
            remote(mine, mine, c, recv, peer(*other)).start()

    def dup_send(c):
        mine = dup_at(c, place)
        remote(mine, mine, c, r_dx.at[c], to_xl).start()
        for other in others[:3]:
            remote(mine, mine, c, r_dup.at[c], peer(*other)).start()

    def dup_pass(c):
        theirs = dup_at(c, (1 - xl) * N_Y + y)
        arrived(theirs, r_dx.at[c])
        for other in others[:3]:
            remote(theirs, theirs, c, r_dup.at[c], peer(*other)).start()

    def dup_share(c):
        arrived(dup_v.at[pl.ds(c * 16 + core * PLANE, PLANE - 2)], r_dup.at[c])
        half = dup_v.at[pl.ds(c * 16 + core * PLANE, PLANE)]
        remote(half, half, c, r_sib.at[c], to_sib).start()

    def inner_form(c):
        arrived(dup_v.at[pl.ds(c * 16 + (1 - core) * PLANE, PLANE)], r_sib.at[c])
        d_up = dup_v[pl.ds(c * 16, 16)].reshape(16 * TB, W)
        for half in (1 - xh, xh):
            lhs = xt_v[half].reshape(N_Z * RB, 16 * TB)
            grad = jnp.dot(lhs, d_up, preferred_element_type=F32)
            for rel in range(N_Z):
                block = half * N_Z + lax.rem(z + rel, N_Z)
                w_part = w_v[c, block].astype(F32)
                inner_v[c, half, rel] = (
                    w_part - inner_rate * grad[rel * RB : (rel + 1) * RB]
                ).astype(BF16)

    def add_into(dst, other):
        dst[...] = (dst[...].astype(F32) + other[...].astype(F32)).astype(BF16)

    def z_first(c):
        remote(inner_v.at[c, 0, 2], r1_v.at[c, 0], c, r_s1.at[c, 0], to_up).start()
        remote(inner_v.at[c, 1, 2], r1_v.at[c, 1], c, r_s1.at[c, 1], to_dn).start()
        remote(inner_v.at[c, 1, 1], r2_v.at[c, 0, 1], c, r_raw.at[c, 0], to_up).start()
        remote(inner_v.at[c, 0, 3], r2_v.at[c, 1, 0], c, r_raw.at[c, 1], to_dn).start()

    def z_second(c):
        arrived(r1_v.at[c, 0], r_s1.at[c, 0])
        add_into(inner_v.at[c, 0, 1], r1_v.at[c, 0])
        remote(inner_v.at[c, 0, 1], r2_v.at[c, 0, 0], c, r_acc.at[c, 0], to_up).start()
        arrived(r1_v.at[c, 1], r_s1.at[c, 1])
        add_into(inner_v.at[c, 1, 3], r1_v.at[c, 1])
        remote(inner_v.at[c, 1, 3], r2_v.at[c, 1, 1], c, r_acc.at[c, 1], to_dn).start()

    def z_third(c):
        arrived(r2_v.at[c, 0, 1], r_raw.at[c, 0])
        arrived(r2_v.at[c, 1, 0], r_raw.at[c, 1])
        arrived(r2_v.at[c, 0, 0], r_acc.at[c, 0])
        arrived(r2_v.at[c, 1, 1], r_acc.at[c, 1])
        xs_v[c] = (
            inner_v[c, 1 - xh, 0].astype(F32)
            + r2_v[c, 0, 1 - xh].astype(F32)
            + r2_v[c, 1, 1 - xh].astype(F32)
        ).astype(BF16)
        remote(xs_v.at[c], rx_v.at[c], c, r_x.at[c], to_x).start()

    def x_first(c):
        remote(inner_v.at[c, 1 - xh], rxx_v.at[x_slot(c)], c, r_x.at[c], to_x).start()

    def x_second(c):
        got = rxx_v.at[x_slot(c)]
        arrived(got, r_x.at[c])
        low, high = pl.ds(0, HB), pl.ds(HB, HB)
        far, above, below = (inner_v.at[c, xh, rel] for rel in (2, 1, 3))
        add_into(far, got.at[2])
        remote(far.at[low], r1_v.at[c, 0, low], c, r_s1.at[c, 0], to_up).start()
        remote(far.at[high], r1_v.at[c, 1, low], c, r_s1.at[c, 1], to_dn).start()
        add_into(above, got.at[1])
        remote(above.at[high], r2_v.at[c, 0, 0, high], c, r_raw.at[c, 0], to_up).start()
        add_into(below, got.at[3])
        remote(below.at[low], r2_v.at[c, 1, 0, low], c, r_raw.at[c, 1], to_dn).start()

    def x_third(c):
        low, high = pl.ds(0, HB), pl.ds(HB, HB)
        arrived(r1_v.at[c, 0, low], r_s1.at[c, 0])
        above = inner_v.at[c, xh, 1, low]
        add_into(above, r1_v.at[c, 0, low])
        remote(above, r2_v.at[c, 0, 0, low], c, r_acc.at[c, 0], to_up).start()
        arrived(r1_v.at[c, 1, low], r_s1.at[c, 1])
        below = inner_v.at[c, xh, 3, high]
        add_into(below, r1_v.at[c, 1, low])
        remote(below, r2_v.at[c, 1, 0, high], c, r_acc.at[c, 1], to_dn).start()

    def block_of(c, half, zz):
        return nw_out.at[c, half * N_Z + zz]

    def update(c, total):
        own = outer_v[:, cols(c)]
        delta = own - total * (1.0 / N_ISL)
        moment = nesterov_mu * mom_v[:, cols(c)] + delta
        new = own - outer_rate * (delta + nesterov_mu * moment)
        nm_out[:, cols(c)] = moment
        no_out[:, cols(c)] = new
        nw_out[c, isl] = new.astype(BF16)
        mine = block_of(c, xh, z)
        remote(mine, mine, c, r_gx.at[c], to_x).start()
        remote(mine, mine, c, r_go.at[c, 0], to_up).start()
        remote(mine, mine, c, r_go.at[c, 1], to_dn).start()

    def z_update(c):
        arrived(rx_v.at[c], r_x.at[c])
        update(
            c,
            inner_v[c, xh, 0].astype(F32)
            + r2_v[c, 0, xh].astype(F32)
            + r2_v[c, 1, xh].astype(F32)
            + rx_v[c].astype(F32),
        )

    def x_update(c):
        half = pl.ds(0, HB)
        arrived(r2_v.at[c, 0, 0, half], r_raw.at[c, 0])
        arrived(r2_v.at[c, 1, 0, half], r_raw.at[c, 1])
        arrived(r2_v.at[c, 0, 0, half], r_acc.at[c, 0])
        arrived(r2_v.at[c, 1, 0, half], r_acc.at[c, 1])
        update(
            c,
            inner_v[c, xh, 0].astype(F32)
            + rxx_v[x_slot(c), 0].astype(F32)
            + r2_v[c, 0, 0].astype(F32)
            + r2_v[c, 1, 0].astype(F32),
        )

    def z_partner(c):
        theirs = block_of(c, 1 - xh, z)
        arrived(theirs, r_gx.at[c])
        remote(theirs, theirs, c, r_gp.at[c, 0], to_up).start()
        remote(theirs, theirs, c, r_gp.at[c, 1], to_dn).start()

    def z_forward(c):
        arrived(block_of(c, xh, dn_z), r_go.at[c, 0])
        arrived(block_of(c, 1 - xh, dn_z), r_gp.at[c, 0])
        low = block_of(c, 0, dn_z)
        remote(low, low, c, r_gf.at[c, 0], to_up).start()
        arrived(block_of(c, xh, up_z), r_go.at[c, 1])
        arrived(block_of(c, 1 - xh, up_z), r_gp.at[c, 1])
        high = block_of(c, 1, up_z)
        remote(high, high, c, r_gf.at[c, 1], to_dn).start()

    def z_last(c):
        arrived(block_of(c, 0, op_z), r_gf.at[c, 0])
        arrived(block_of(c, 1, op_z), r_gf.at[c, 1])

    def half_of(c, half, zz, part):
        return nw_out.at[c, half * N_Z + zz, pl.ds(part * HB, HB)]

    def x_neighbours(c):
        below = block_of(c, xh, dn_z)
        arrived(below, r_go.at[c, 0])
        part = half_of(c, xh, dn_z, 0)
        remote(part, part, c, r_gf.at[c, 0], to_up).start()
        remote(below, below, c, r_gp.at[c, 0], to_x).start()
        above = block_of(c, xh, up_z)
        arrived(above, r_go.at[c, 1])
        part = half_of(c, xh, up_z, 1)
        remote(part, part, c, r_gf.at[c, 1], to_dn).start()
        remote(above, above, c, r_gp.at[c, 1], to_x).start()

    def x_far(c):
        arrived(half_of(c, xh, op_z, 0), r_gf.at[c, 0])
        arrived(half_of(c, xh, op_z, 1), r_gf.at[c, 1])
        far = block_of(c, xh, op_z)
        remote(far, far, c, r_gz.at[c], to_x).start()

    def x_last(c):
        arrived(block_of(c, 1 - xh, z), r_gx.at[c])
        arrived(block_of(c, 1 - xh, dn_z), r_gp.at[c, 0])
        arrived(block_of(c, 1 - xh, up_z), r_gp.at[c, 1])
        arrived(block_of(c, 1 - xh, op_z), r_gz.at[c])

    def either(z_step, x_step):
        def step(c):
            is_x = functools.reduce(jnp.logical_or, [c == k for k in X_CHUNKS])

            @pl.when(is_x)
            def _():
                x_step(c)

            @pl.when(jnp.logical_not(is_x))
            def _():
                z_step(c)

        return step

    def up_form(c):
        w_all = w_v[c].reshape(N_ISL * RB, W)
        lhs = x_v[1 - core].reshape(PLANE * TB, N_ISL * RB)
        ups_v[c] = jnp.dot(lhs, w_all, preferred_element_type=F32).astype(BF16)
        remote(ups_v.at[c], upr_v.at[c], c, r_ups.at[c], to_sib).start()
        lhs = x_v[core].reshape(PLANE * TB, N_ISL * RB)
        upo_v[c] = jnp.dot(lhs, w_all, preferred_element_type=F32).astype(BF16)

    def up_add(c):
        arrived(upr_v.at[c], r_ups.at[c])
        both = upo_v[c].astype(F32) + upr_v[c].astype(F32)
        upt_v[c] = both.astype(BF16).reshape(2, N_Y, TB, W)
        for k in (1, 2, 3):
            to = along_y(k)
            remote(
                upt_v.at[c, :, to], upp_v.at[c, y], c, r_upp.at[c], peer(xl, to)
            ).start()

    def up_cross(c):
        arrived(upp_v.at[c, pl.ds(0, N_Y - 1)], r_upp.at[c])
        total = upt_v[c, :, y].astype(F32)
        for k in (1, 2, 3):
            total = total + upp_v[c, along_y(k)].astype(F32)
        upy_v[c] = total.astype(BF16)
        remote(upy_v.at[c, 1 - xl], upx_v.at[c], c, r_upx.at[c], to_xl).start()

    def up_last(c):
        arrived(upx_v.at[c], r_upx.at[c])
        up = upy_v[c, xl].astype(F32) + upx_v[c].astype(F32)
        g = gate_v[:, cols(c)].astype(F32)
        s = jax.nn.sigmoid(g)
        out = cot_v[:, cols(c)].astype(F32) * up * s * (1.0 + g * (1.0 - s))
        gg_out[:, cols(c)] = out.astype(BF16)

    def ig_form(c):
        d_up = dup_v[pl.ds(c * 16, 16)].reshape(16 * TB, W)
        w_all = w_v[c].reshape(N_ISL * RB, W)
        part = lax.dot_general(
            d_up, w_all, (((1,), (1,)), ((), ())), preferred_element_type=F32
        )
        acc_v[...] += part

    in_copies[0].wait()
    in_copies[1].wait()
    @pl.loop(0, n_chunk)
    def _(c):
        dup_form(c)

    pl.semaphore_wait(barrier, 4 + PLANE - 1)
    for c in range(FIRST):
        dup_send_all(c)

    @pl.loop(FIRST, n_chunk)
    def _(c):
        dup_send(c)

    w_copy(0).start()
    in_copies[2].wait()
    in_copies[3].wait()
    for block in range(N_ISL):
        piece = x_v[:, :, :, block * RB : (block + 1) * RB].reshape(16 * TB, RB)
        rel = lax.rem(block % N_Z + N_Z - z, N_Z)
        xt_v[block // N_Z, rel] = piece.T
    for c in range(FIRST):
        arrived(dup_at(c, (1 - xl) * N_Y + y), r_dx.at[c])
        dup_share(c)

    @pl.loop(1, n_chunk)
    def _(c):
        w_copy(c).start()

    @pl.loop(FIRST, max(FIRST, AHEAD_B))
    def _(c):
        dup_pass(c)

    in_copies[4].start()
    in_copies[5].start()
    acc_v[...] = jnp.zeros_like(acc_v)

    def at(c, lo, hi, *steps):
        @pl.when((c >= lo) & (c < hi))
        def _():
            for step in steps:
                step(c)

    @pl.loop(0, n_chunk + LAG_F)
    def _(t):
        def start_sum(c):
            w_copy(c).wait()
            inner_form(c)
            either(z_first, x_first)(c)
            up_form(c)

        at(t, 0, n_chunk, start_sum)

        at(t + AHEAD_B, max(FIRST, AHEAD_B), n_chunk, dup_pass)
        at(t + AHEAD_C, FIRST, n_chunk, dup_share)
        at(t - LAG_A, 0, n_chunk, either(z_second, x_second))
        at(t - LAG_B, 0, n_chunk, either(z_third, x_third))

        @pl.when(t == LAG_C)
        def _():
            in_copies[4].wait()
            in_copies[5].wait()

        at(t - LAG_C, 0, n_chunk, either(z_update, x_update))
        at(t - LAG_D, 0, n_chunk, either(z_partner, x_neighbours))
        at(t - LAG_E, 0, n_chunk, either(z_forward, x_far))
        at(t, 0, n_chunk, ig_form)

        @pl.when(t == n_chunk + LAG_A)
        def _():
            for half in range(2):
                rows = acc_v[half * PLANE * TB : (half + 1) * PLANE * TB].astype(BF16)
                ig_out[:, half] = rows.reshape(PLANE, TB, N_ISL * RB)

        at(t - LAG_UA, 0, n_chunk, up_add)
        at(t - LAG_UB, 0, n_chunk, up_cross)
        at(t - LAG_UC, 0, n_chunk, up_last)
        at(t - LAG_F, 0, n_chunk, either(z_last, x_last))

    sent = (2 * 7 * TB + 2 * PLANE * TB + 6 * RB + RB + 3 * RB + 2 * RB + 2 * RB) // TB

    @pl.loop(0, n_chunk)
    def _(c):
        arrived(dup_v.at[pl.ds(0, sent)], snd.at[c])


def write_out(ig, gg, nw, no, nm, ig_out, gg_out, nw_out, no_out, nm_out, sem):
    pairs = [(nw.at[c], nw_out.at[:, :, c * W : (c + 1) * W]) for c in range(nw.shape[0])]
    pairs += [(no, no_out), (nm, nm_out), (ig, ig_out), (gg, gg_out)]
    copies = [
        pltpu.make_async_copy(src, dst, sem.at[k]) for k, (src, dst) in enumerate(pairs)
    ]
    for copy in copies:
        copy.start()
    for copy in copies:
        copy.wait()


def local(inputs, gate_pre, up_cot, weights, outer, momentum):
    d_loc, fs = weights.shape[1], weights.shape[2]
    tok = inputs.shape[1]
    c = fs // W
    dma = pltpu.SemaphoreType.DMA
    vmem = pl.BlockSpec(memory_space=pltpu.VMEM)
    hbm = pl.BlockSpec(memory_space=pltpu.HBM)
    results = pl.pallas_call(
        functools.partial(kernel, c),
        out_shape=(
            pltpu.VMEM((PLANE, 2, TB, d_loc), BF16),
            pltpu.VMEM((TB, fs), BF16),
            pltpu.VMEM((c, N_ISL, RB, W), BF16),
            pltpu.VMEM((RB, fs), F32),
            pltpu.VMEM((RB, fs), F32),
        ),
        in_specs=[hbm] * 6,
        out_specs=(vmem,) * 5,
        scratch_shapes=[
            pltpu.VMEM((2, PLANE, TB, d_loc), BF16),
            pltpu.VMEM((2, N_Z, RB, tok), BF16),
            pltpu.VMEM((TB, fs), BF16),
            pltpu.VMEM((TB, fs), BF16),
            pltpu.VMEM((RB, fs), F32),
            pltpu.VMEM((RB, fs), F32),
            pltpu.VMEM((c, N_ISL, RB, W), BF16),
            pltpu.VMEM((c * 16, TB, W), BF16),
            pltpu.VMEM((c, 2, N_Z, RB, W), BF16),
            pltpu.VMEM((c, 2, RB, W), BF16),
            pltpu.VMEM((c, 2, 2, RB, W), BF16),
            pltpu.VMEM((c, RB, W), BF16),
            pltpu.VMEM((c, RB, W), BF16),
            pltpu.VMEM((len(X_CHUNKS), N_Z, RB, W), BF16),
            pltpu.VMEM((c, PLANE * TB, W), BF16),
            pltpu.VMEM((c, PLANE * TB, W), BF16),
            pltpu.VMEM((c, PLANE * TB, W), BF16),
            pltpu.VMEM((c, 2, N_Y, TB, W), BF16),
            pltpu.VMEM((c, N_Y, 2, TB, W), BF16),
            pltpu.VMEM((c, TB, W), BF16),
            pltpu.VMEM((c, 2, TB, W), BF16),
            pltpu.VMEM((tok, d_loc), F32),
            dma((6,)),
            dma((c,)),
            dma((c,)),
            dma((c,)),
            dma((c,)),
            dma((c,)),
            dma((c, 2)),
            dma((c, 2)),
            dma((c, 2)),
            dma((c,)),
            dma((c,)),
            dma((c, 2)),
            dma((c, 2)),
            dma((c, 2)),
            dma((c,)),
            dma((c,)),
            dma((c,)),
            dma((c,)),
        ],
        compiler_params=pltpu.CompilerParams(
            collective_id=0, has_side_effects=True, vmem_limit_bytes=48 * 2**20
        ),
        cost_estimate=pl.CostEstimate(
            flops=6 * tok * d_loc * fs, bytes_accessed=8 * d_loc * fs, transcendentals=0
        ),
    )(
        inputs.reshape(PLANE, 2, TB, d_loc),
        gate_pre[0],
        up_cot[0],
        weights.reshape(N_ISL, RB, fs),
        outer,
        momentum,
    )
    ig, gg, nw, no, nm = pl.pallas_call(
        write_out,
        out_shape=(
            jax.ShapeDtypeStruct((PLANE, 2, TB, d_loc), BF16),
            jax.ShapeDtypeStruct((TB, fs), BF16),
            jax.ShapeDtypeStruct((N_ISL, RB, fs), BF16),
            jax.ShapeDtypeStruct((RB, fs), F32),
            jax.ShapeDtypeStruct((RB, fs), F32),
        ),
        in_specs=[vmem] * 5,
        out_specs=(hbm,) * 5,
        scratch_shapes=[dma((c + 4,))],
        compiler_params=pltpu.CompilerParams(vmem_limit_bytes=2 * 2**20),
    )(*results)
    return (
        ig.reshape(1, tok, d_loc),
        gg[None],
        nw.reshape(d_loc, fs),
        no,
        nm,
    )


def solution(mesh):
    placed = (
        P("island", None, "section"),
        P("island", "section", None),
        P("island", "section", None),
        P("island", "section", None),
        P(("section", "island"), None),
        P(("section", "island"), None),
    )
    return jax.shard_map(
        local,
        mesh=mesh,
        in_specs=placed,
        out_specs=(
            P("island", None, "section"),
            P("island", "section", None),
            P("section", None),
            P(("section", "island"), None),
            P(("section", "island"), None),
        ),
        check_vma=False,
    )
```

```python
import functools

import jax
import jax.numpy as jnp
from jax import lax
from jax.experimental import pallas as pl
from jax.experimental.pallas import tpu as pltpu
from jax.sharding import PartitionSpec as P

inner_rate = 0.0005
outer_rate = 0.7
nesterov_mu = 0.9

MESH = pl.DeviceIdType.MESH
F32 = jnp.float32
BF16 = jnp.bfloat16

W = 256
N_Z = 4
N_ISL = 8
N_Y = 4
PLANE = 8
TB = 32
RB = 128
HB = RB // 2
X_CHUNKS = (1, 4, 6, 9, 11)
LAG_A, LAG_B, LAG_C, LAG_D, LAG_E, LAG_F = 2, 4, 6, 10, 14, 18
LAG_UA, LAG_UB, LAG_UC = 6, 9, 14
AHEAD_B, AHEAD_C = 2, 1
FIRST = 3
EARLY = 2


def kernel(
    n_chunk,
    x_hbm, gate_hbm, cot_hbm, w_hbm, outer_hbm, mom_hbm,
    ig_out, gg_out, nw_out, no_out, nm_out,
    x_v, xt_v, gate_v, cot_v, outer_v, mom_v, w_v, dup_v,
    inner_v, r1_v, r2_v, xs_v, rx_v, rxx_v,
    ups_v, upr_v, upo_v, upt_v, upp_v, upx_v, upy_v, acc_v,
    in_sem, w_sem, snd, r_dup, r_dx, r_sib, r_s1, r_raw, r_acc, r_x,
    r_gx, r_go, r_gp, r_gf, r_gz, r_ups, r_upp, r_upx,
):
    sec = lax.axis_index("section")
    isl = lax.axis_index("island")
    core = lax.rem(sec, 2)
    place = sec // 2
    xl = place // N_Y
    y = lax.rem(place, N_Y)
    z = lax.rem(isl, N_Z)
    xh = isl // N_Z
    up_z = lax.rem(z + 1, N_Z)
    dn_z = lax.rem(z + N_Z - 1, N_Z)
    op_z = lax.rem(z + 2, N_Z)
    to_up = (sec, xh * N_Z + up_z)
    to_dn = (sec, xh * N_Z + dn_z)
    to_x = (sec, (1 - xh) * N_Z + z)
    to_sib = (place * 2 + 1 - core, isl)

    to_xl = (((1 - xl) * N_Y + y) * 2 + core, isl)

    def along_y(k):
        return lax.rem(y + k, N_Y)

    def peer(x_at, y_at):
        return ((x_at * N_Y + y_at) * 2 + core, isl)

    def remote(src, dst, c, recv, device):
        return pltpu.make_async_remote_copy(
            src_ref=src, dst_ref=dst, send_sem=snd.at[c], recv_sem=recv,
            device_id=device, device_id_type=MESH,
        )

    def arrived(dst, recv):
        pltpu.make_async_copy(dst, dst, recv).wait()

    def x_slot(c):
        return sum((c > k).astype(jnp.int32) for k in X_CHUNKS)

    def cols(c):
        return pl.ds(pl.multiple_of(c * W, W), W)

    barrier = pltpu.get_barrier_semaphore()
    others = [(xl, along_y(k)) for k in (1, 2, 3)]
    others += [(1 - xl, along_y(k)) for k in (0, 1, 2, 3)]
    for device in [peer(*other) for other in others] + [to_sib, to_up, to_dn, to_x]:
        pl.semaphore_signal(barrier, inc=1, device_id=device, device_id_type=MESH)

    def w_copy(c):
        return pltpu.make_async_copy(w_hbm.at[:, :, cols(c)], w_v.at[c], w_sem.at[c])

    in_copies = [
        pltpu.make_async_copy(gate_hbm, gate_v, in_sem.at[0]),
        pltpu.make_async_copy(cot_hbm, cot_v, in_sem.at[1]),
        pltpu.make_async_copy(x_hbm.at[:, 0], x_v.at[0], in_sem.at[2]),
        pltpu.make_async_copy(x_hbm.at[:, 1], x_v.at[1], in_sem.at[3]),
        pltpu.make_async_copy(outer_hbm, outer_v, in_sem.at[4]),
        pltpu.make_async_copy(mom_hbm, mom_v, in_sem.at[5]),
    ]
    for copy in in_copies[:4]:
        copy.start()

    def dup_form(c):
        g = gate_v[:, cols(c)].astype(F32)
        s = jax.nn.sigmoid(g)
        d = cot_v[:, cols(c)].astype(F32) * g * s
        dup_v[c * 16 + core * PLANE + place] = d.astype(BF16)

    def dup_at(c, p):
        return dup_v.at[c * 16 + core * PLANE + p]

    def dup_send_all(c):
        mine = dup_at(c, place)
        for other in others:
            recv = r_dx.at[c] if other is others[3] else r_dup.at[c]
            remote(mine, mine, c, recv, peer(*other)).start()

    def dup_send(c):
        mine = dup_at(c, place)
        remote(mine, mine, c, r_dx.at[c], to_xl).start()
        for other in others[:3]:
            remote(mine, mine, c, r_dup.at[c], peer(*other)).start()

    def dup_pass(c):
        theirs = dup_at(c, (1 - xl) * N_Y + y)
        arrived(theirs, r_dx.at[c])
        for other in others[:3]:
            remote(theirs, theirs, c, r_dup.at[c], peer(*other)).start()

    def dup_share(c):
        arrived(dup_v.at[pl.ds(c * 16 + core * PLANE, PLANE - 2)], r_dup.at[c])
        half = dup_v.at[pl.ds(c * 16 + core * PLANE, PLANE)]
        remote(half, half, c, r_sib.at[c], to_sib).start()

    def inner_form(c):
        arrived(dup_v.at[pl.ds(c * 16 + (1 - core) * PLANE, PLANE)], r_sib.at[c])
        d_up = dup_v[pl.ds(c * 16, 16)].reshape(16 * TB, W)
        for half in (1 - xh, xh):
            lhs = xt_v[half].reshape(N_Z * RB, 16 * TB)
            grad = jnp.dot(lhs, d_up, preferred_element_type=F32)
            for rel in range(N_Z):
                block = half * N_Z + lax.rem(z + rel, N_Z)
                w_part = w_v[c, block].astype(F32)
                inner_v[c, half, rel] = (
                    w_part - inner_rate * grad[rel * RB : (rel + 1) * RB]
                ).astype(BF16)

    def add_into(dst, other):
        dst[...] = (dst[...].astype(F32) + other[...].astype(F32)).astype(BF16)

    def z_first(c):
        remote(inner_v.at[c, 0, 2], r1_v.at[c, 0], c, r_s1.at[c, 0], to_up).start()
        remote(inner_v.at[c, 1, 2], r1_v.at[c, 1], c, r_s1.at[c, 1], to_dn).start()
        remote(inner_v.at[c, 1, 1], r2_v.at[c, 0, 1], c, r_raw.at[c, 0], to_up).start()
        remote(inner_v.at[c, 0, 3], r2_v.at[c, 1, 0], c, r_raw.at[c, 1], to_dn).start()

    def z_second(c):
        arrived(r1_v.at[c, 0], r_s1.at[c, 0])
        add_into(inner_v.at[c, 0, 1], r1_v.at[c, 0])
        remote(inner_v.at[c, 0, 1], r2_v.at[c, 0, 0], c, r_acc.at[c, 0], to_up).start()
        arrived(r1_v.at[c, 1], r_s1.at[c, 1])
        add_into(inner_v.at[c, 1, 3], r1_v.at[c, 1])
        remote(inner_v.at[c, 1, 3], r2_v.at[c, 1, 1], c, r_acc.at[c, 1], to_dn).start()

    def z_third(c):
        arrived(r2_v.at[c, 0, 1], r_raw.at[c, 0])
        arrived(r2_v.at[c, 1, 0], r_raw.at[c, 1])
        arrived(r2_v.at[c, 0, 0], r_acc.at[c, 0])
        arrived(r2_v.at[c, 1, 1], r_acc.at[c, 1])
        xs_v[c] = (
            inner_v[c, 1 - xh, 0].astype(F32)
            + r2_v[c, 0, 1 - xh].astype(F32)
            + r2_v[c, 1, 1 - xh].astype(F32)
        ).astype(BF16)
        remote(xs_v.at[c], rx_v.at[c], c, r_x.at[c], to_x).start()

    def x_first(c):
        remote(inner_v.at[c, 1 - xh], rxx_v.at[x_slot(c)], c, r_x.at[c], to_x).start()

    def x_second(c):
        got = rxx_v.at[x_slot(c)]
        arrived(got, r_x.at[c])
        low, high = pl.ds(0, HB), pl.ds(HB, HB)
        far, above, below = (inner_v.at[c, xh, rel] for rel in (2, 1, 3))
        add_into(far, got.at[2])
        remote(far.at[low], r1_v.at[c, 0, low], c, r_s1.at[c, 0], to_up).start()
        remote(far.at[high], r1_v.at[c, 1, low], c, r_s1.at[c, 1], to_dn).start()
        add_into(above, got.at[1])
        remote(above.at[high], r2_v.at[c, 0, 0, high], c, r_raw.at[c, 0], to_up).start()
        add_into(below, got.at[3])
        remote(below.at[low], r2_v.at[c, 1, 0, low], c, r_raw.at[c, 1], to_dn).start()

    def x_third(c):
        low, high = pl.ds(0, HB), pl.ds(HB, HB)
        arrived(r1_v.at[c, 0, low], r_s1.at[c, 0])
        above = inner_v.at[c, xh, 1, low]
        add_into(above, r1_v.at[c, 0, low])
        remote(above, r2_v.at[c, 0, 0, low], c, r_acc.at[c, 0], to_up).start()
        arrived(r1_v.at[c, 1, low], r_s1.at[c, 1])
        below = inner_v.at[c, xh, 3, high]
        add_into(below, r1_v.at[c, 1, low])
        remote(below, r2_v.at[c, 1, 0, high], c, r_acc.at[c, 1], to_dn).start()

    def block_of(c, half, zz):
        return nw_out.at[c, half * N_Z + zz]

    def update(c, total):
        own = outer_v[:, cols(c)]
        delta = own - total * (1.0 / N_ISL)
        moment = nesterov_mu * mom_v[:, cols(c)] + delta
        new = own - outer_rate * (delta + nesterov_mu * moment)
        nm_out[:, cols(c)] = moment
        no_out[:, cols(c)] = new
        nw_out[c, isl] = new.astype(BF16)
        mine = block_of(c, xh, z)
        remote(mine, mine, c, r_gx.at[c], to_x).start()
        remote(mine, mine, c, r_go.at[c, 0], to_up).start()
        remote(mine, mine, c, r_go.at[c, 1], to_dn).start()

    def z_update(c):
        arrived(rx_v.at[c], r_x.at[c])
        update(
            c,
            inner_v[c, xh, 0].astype(F32)
            + r2_v[c, 0, xh].astype(F32)
            + r2_v[c, 1, xh].astype(F32)
            + rx_v[c].astype(F32),
        )

    def x_update(c):
        half = pl.ds(0, HB)
        arrived(r2_v.at[c, 0, 0, half], r_raw.at[c, 0])
        arrived(r2_v.at[c, 1, 0, half], r_raw.at[c, 1])
        arrived(r2_v.at[c, 0, 0, half], r_acc.at[c, 0])
        arrived(r2_v.at[c, 1, 0, half], r_acc.at[c, 1])
        update(
            c,
            inner_v[c, xh, 0].astype(F32)
            + rxx_v[x_slot(c), 0].astype(F32)
            + r2_v[c, 0, 0].astype(F32)
            + r2_v[c, 1, 0].astype(F32),
        )

    def z_partner(c):
        theirs = block_of(c, 1 - xh, z)
        arrived(theirs, r_gx.at[c])
        remote(theirs, theirs, c, r_gp.at[c, 0], to_up).start()
        remote(theirs, theirs, c, r_gp.at[c, 1], to_dn).start()

    def z_forward(c):
        arrived(block_of(c, xh, dn_z), r_go.at[c, 0])
        arrived(block_of(c, 1 - xh, dn_z), r_gp.at[c, 0])
        low = block_of(c, 0, dn_z)
        remote(low, low, c, r_gf.at[c, 0], to_up).start()
        arrived(block_of(c, xh, up_z), r_go.at[c, 1])
        arrived(block_of(c, 1 - xh, up_z), r_gp.at[c, 1])
        high = block_of(c, 1, up_z)
        remote(high, high, c, r_gf.at[c, 1], to_dn).start()

    def z_last(c):
        arrived(block_of(c, 0, op_z), r_gf.at[c, 0])
        arrived(block_of(c, 1, op_z), r_gf.at[c, 1])

    def half_of(c, half, zz, part):
        return nw_out.at[c, half * N_Z + zz, pl.ds(part * HB, HB)]

    def x_neighbours(c):
        below = block_of(c, xh, dn_z)
        arrived(below, r_go.at[c, 0])
        part = half_of(c, xh, dn_z, 0)
        remote(part, part, c, r_gf.at[c, 0], to_up).start()
        remote(below, below, c, r_gp.at[c, 0], to_x).start()
        above = block_of(c, xh, up_z)
        arrived(above, r_go.at[c, 1])
        part = half_of(c, xh, up_z, 1)
        remote(part, part, c, r_gf.at[c, 1], to_dn).start()
        remote(above, above, c, r_gp.at[c, 1], to_x).start()

    def x_far(c):
        arrived(half_of(c, xh, op_z, 0), r_gf.at[c, 0])
        arrived(half_of(c, xh, op_z, 1), r_gf.at[c, 1])
        far = block_of(c, xh, op_z)
        remote(far, far, c, r_gz.at[c], to_x).start()

    def x_last(c):
        arrived(block_of(c, 1 - xh, z), r_gx.at[c])
        arrived(block_of(c, 1 - xh, dn_z), r_gp.at[c, 0])
        arrived(block_of(c, 1 - xh, up_z), r_gp.at[c, 1])
        arrived(block_of(c, 1 - xh, op_z), r_gz.at[c])

    def either(z_step, x_step):
        def step(c):
            is_x = functools.reduce(jnp.logical_or, [c == k for k in X_CHUNKS])

            @pl.when(is_x)
            def _():
                x_step(c)

            @pl.when(jnp.logical_not(is_x))
            def _():
                z_step(c)

        return step

    def up_form(c):
        w_all = w_v[c].reshape(N_ISL * RB, W)
        lhs = x_v[1 - core].reshape(PLANE * TB, N_ISL * RB)
        ups_v[c] = jnp.dot(lhs, w_all, preferred_element_type=F32).astype(BF16)
        remote(ups_v.at[c], upr_v.at[c], c, r_ups.at[c], to_sib).start()
        lhs = x_v[core].reshape(PLANE * TB, N_ISL * RB)
        upo_v[c] = jnp.dot(lhs, w_all, preferred_element_type=F32).astype(BF16)

    def up_add(c):
        arrived(upr_v.at[c], r_ups.at[c])
        both = upo_v[c].astype(F32) + upr_v[c].astype(F32)
        upt_v[c] = both.astype(BF16).reshape(2, N_Y, TB, W)
        for k in (1, 2, 3):
            to = along_y(k)
            remote(
                upt_v.at[c, :, to], upp_v.at[c, y], c, r_upp.at[c], peer(xl, to)
            ).start()

    def up_cross(c):
        arrived(upp_v.at[c, pl.ds(0, N_Y - 1)], r_upp.at[c])
        total = upt_v[c, :, y].astype(F32)
        for k in (1, 2, 3):
            total = total + upp_v[c, along_y(k)].astype(F32)
        upy_v[c] = total.astype(BF16)
        remote(upy_v.at[c, 1 - xl], upx_v.at[c], c, r_upx.at[c], to_xl).start()

    def up_last(c):
        arrived(upx_v.at[c], r_upx.at[c])
        up = upy_v[c, xl].astype(F32) + upx_v[c].astype(F32)
        g = gate_v[:, cols(c)].astype(F32)
        s = jax.nn.sigmoid(g)
        out = cot_v[:, cols(c)].astype(F32) * up * s * (1.0 + g * (1.0 - s))
        gg_out[:, cols(c)] = out.astype(BF16)

    def ig_form(c):
        d_up = dup_v[pl.ds(c * 16, 16)].reshape(16 * TB, W)
        w_all = w_v[c].reshape(N_ISL * RB, W)
        part = lax.dot_general(
            d_up, w_all, (((1,), (1,)), ((), ())), preferred_element_type=F32
        )
        acc_v[...] += part

    in_copies[0].wait()
    in_copies[1].wait()
    @pl.loop(0, n_chunk)
    def _(c):
        dup_form(c)

    pl.semaphore_wait(barrier, 4 + PLANE - 1)
    for c in range(FIRST):
        dup_send_all(c)

    @pl.loop(FIRST, n_chunk)
    def _(c):
        dup_send(c)

    w_copy(0).start()
    in_copies[2].wait()
    in_copies[3].wait()
    for block in range(N_ISL):
        piece = x_v[:, :, :, block * RB : (block + 1) * RB].reshape(16 * TB, RB)
        rel = lax.rem(block % N_Z + N_Z - z, N_Z)
        xt_v[block // N_Z, rel] = piece.T
    def share_first(c):
        arrived(dup_at(c, (1 - xl) * N_Y + y), r_dx.at[c])
        dup_share(c)

    for c in range(EARLY):
        share_first(c)

    @pl.loop(1, n_chunk)
    def _(c):
        w_copy(c).start()

    @pl.loop(FIRST, max(FIRST, AHEAD_B))
    def _(c):
        dup_pass(c)

    in_copies[4].start()
    in_copies[5].start()
    acc_v[...] = jnp.zeros_like(acc_v)

    def at(c, lo, hi, *steps):
        @pl.when((c >= lo) & (c < hi))
        def _():
            for step in steps:
                step(c)

    @pl.loop(0, n_chunk + LAG_F)
    def _(t):
        def start_sum(c):
            w_copy(c).wait()
            inner_form(c)
            either(z_first, x_first)(c)
            up_form(c)

        at(t, 0, n_chunk, start_sum)

        at(t + AHEAD_B, max(FIRST, AHEAD_B), n_chunk, dup_pass)
        at(t + AHEAD_C, EARLY, FIRST, share_first)
        at(t + AHEAD_C, FIRST, n_chunk, dup_share)
        at(t - LAG_A, 0, n_chunk, either(z_second, x_second))
        at(t - LAG_B, 0, n_chunk, either(z_third, x_third))

        @pl.when(t == LAG_C)
        def _():
            in_copies[4].wait()
            in_copies[5].wait()

        at(t - LAG_C, 0, n_chunk, either(z_update, x_update))
        at(t - LAG_D, 0, n_chunk, either(z_partner, x_neighbours))
        at(t - LAG_E, 0, n_chunk, either(z_forward, x_far))
        at(t, 0, n_chunk, ig_form)

        @pl.when(t == n_chunk + LAG_A)
        def _():
            for half in range(2):
                rows = acc_v[half * PLANE * TB : (half + 1) * PLANE * TB].astype(BF16)
                ig_out[:, half] = rows.reshape(PLANE, TB, N_ISL * RB)

        at(t - LAG_UA, 0, n_chunk, up_add)
        at(t - LAG_UB, 0, n_chunk, up_cross)
        at(t - LAG_UC, 0, n_chunk, up_last)
        at(t - LAG_F, 0, n_chunk, either(z_last, x_last))

    sent = (2 * 7 * TB + 2 * PLANE * TB + 6 * RB + RB + 3 * RB + 2 * RB + 2 * RB) // TB

    @pl.loop(0, n_chunk)
    def _(c):
        arrived(dup_v.at[pl.ds(0, sent)], snd.at[c])


def write_out(ig, gg, nw, no, nm, ig_out, gg_out, nw_out, no_out, nm_out, sem):
    pairs = [(nw.at[c], nw_out.at[:, :, c * W : (c + 1) * W]) for c in range(nw.shape[0])]
    pairs += [(no, no_out), (nm, nm_out), (ig, ig_out), (gg, gg_out)]
    copies = [
        pltpu.make_async_copy(src, dst, sem.at[k]) for k, (src, dst) in enumerate(pairs)
    ]
    for copy in copies:
        copy.start()
    for copy in copies:
        copy.wait()


def local(inputs, gate_pre, up_cot, weights, outer, momentum):
    d_loc, fs = weights.shape[1], weights.shape[2]
    tok = inputs.shape[1]
    c = fs // W
    dma = pltpu.SemaphoreType.DMA
    vmem = pl.BlockSpec(memory_space=pltpu.VMEM)
    hbm = pl.BlockSpec(memory_space=pltpu.HBM)
    results = pl.pallas_call(
        functools.partial(kernel, c),
        out_shape=(
            pltpu.VMEM((PLANE, 2, TB, d_loc), BF16),
            pltpu.VMEM((TB, fs), BF16),
            pltpu.VMEM((c, N_ISL, RB, W), BF16),
            pltpu.VMEM((RB, fs), F32),
            pltpu.VMEM((RB, fs), F32),
        ),
        in_specs=[hbm] * 6,
        out_specs=(vmem,) * 5,
        scratch_shapes=[
            pltpu.VMEM((2, PLANE, TB, d_loc), BF16),
            pltpu.VMEM((2, N_Z, RB, tok), BF16),
            pltpu.VMEM((TB, fs), BF16),
            pltpu.VMEM((TB, fs), BF16),
            pltpu.VMEM((RB, fs), F32),
            pltpu.VMEM((RB, fs), F32),
            pltpu.VMEM((c, N_ISL, RB, W), BF16),
            pltpu.VMEM((c * 16, TB, W), BF16),
            pltpu.VMEM((c, 2, N_Z, RB, W), BF16),
            pltpu.VMEM((c, 2, RB, W), BF16),
            pltpu.VMEM((c, 2, 2, RB, W), BF16),
            pltpu.VMEM((c, RB, W), BF16),
            pltpu.VMEM((c, RB, W), BF16),
            pltpu.VMEM((len(X_CHUNKS), N_Z, RB, W), BF16),
            pltpu.VMEM((c, PLANE * TB, W), BF16),
            pltpu.VMEM((c, PLANE * TB, W), BF16),
            pltpu.VMEM((c, PLANE * TB, W), BF16),
            pltpu.VMEM((c, 2, N_Y, TB, W), BF16),
            pltpu.VMEM((c, N_Y, 2, TB, W), BF16),
            pltpu.VMEM((c, TB, W), BF16),
            pltpu.VMEM((c, 2, TB, W), BF16),
            pltpu.VMEM((tok, d_loc), F32),
            dma((6,)),
            dma((c,)),
            dma((c,)),
            dma((c,)),
            dma((c,)),
            dma((c,)),
            dma((c, 2)),
            dma((c, 2)),
            dma((c, 2)),
            dma((c,)),
            dma((c,)),
            dma((c, 2)),
            dma((c, 2)),
            dma((c, 2)),
            dma((c,)),
            dma((c,)),
            dma((c,)),
            dma((c,)),
        ],
        compiler_params=pltpu.CompilerParams(
            collective_id=0, has_side_effects=True, vmem_limit_bytes=48 * 2**20
        ),
        cost_estimate=pl.CostEstimate(
            flops=6 * tok * d_loc * fs, bytes_accessed=8 * d_loc * fs, transcendentals=0
        ),
    )(
        inputs.reshape(PLANE, 2, TB, d_loc),
        gate_pre[0],
        up_cot[0],
        weights.reshape(N_ISL, RB, fs),
        outer,
        momentum,
    )
    ig, gg, nw, no, nm = pl.pallas_call(
        write_out,
        out_shape=(
            jax.ShapeDtypeStruct((PLANE, 2, TB, d_loc), BF16),
            jax.ShapeDtypeStruct((TB, fs), BF16),
            jax.ShapeDtypeStruct((N_ISL, RB, fs), BF16),
            jax.ShapeDtypeStruct((RB, fs), F32),
            jax.ShapeDtypeStruct((RB, fs), F32),
        ),
        in_specs=[vmem] * 5,
        out_specs=(hbm,) * 5,
        scratch_shapes=[dma((c + 4,))],
        compiler_params=pltpu.CompilerParams(vmem_limit_bytes=2 * 2**20),
    )(*results)
    return (
        ig.reshape(1, tok, d_loc),
        gg[None],
        nw.reshape(d_loc, fs),
        no,
        nm,
    )


def solution(mesh):
    placed = (
        P("island", None, "section"),
        P("island", "section", None),
        P("island", "section", None),
        P("island", "section", None),
        P(("section", "island"), None),
        P(("section", "island"), None),
    )
    return jax.shard_map(
        local,
        mesh=mesh,
        in_specs=placed,
        out_specs=(
            P("island", None, "section"),
            P("island", "section", None),
            P("section", None),
            P(("section", "island"), None),
            P(("section", "island"), None),
        ),
        check_vma=False,
    )
```
